256 devices in a mesh: gx: 16 (over z_hi, y, core), gy: 16 (over x, z_lo).
Axes of the slice: x: 4, y: 4, z: 8 (z_hi: 2, z_lo: 4; z = z_hi * 4 + z_lo), core: 2. Of those that a mesh axis runs over, the one named last changes fastest.
Arguments:
- tokens: bfloat16 [768, 16384], P('gy', 'gx'), may hold values from -6 to 6
- gate_weight: bfloat16 [16384, 26624], P('gx', 'gy'), may hold values from -0.046875 to 0.046875
- up_weight: bfloat16 [16384, 26624], P('gx', 'gy'), may hold values from -0.046875 to 0.046875
- down_weight: bfloat16 [26624, 16384], P('gy', 'gx'), may hold values from -0.0390625 to 0.0390625
Outputs:
- mixed: bfloat16 [768, 16384], P('gy', 'gx')
The draws below stay inside these ranges and needn't reach their ends.
All inputs are finite; a program needn't handle non-finite values.
Results may differ from the reference program's by a relative error of at most 0.035.
Values may be sent and summed in bfloat16 or wider, within the bound.
No kernel may reach another device: no remote copies, remote signals or barrier semaphores. Data moves between devices by JAX's collectives and lax.ppermute only.
A program may use at most 64 MiB of HBM per device.

```python
import jax
import jax.numpy as jnp
from jax import lax

D = 16384
FF = 26624
TOKENS = 768
N_GX = 16
N_GY = 16


def block_scale(rng, dims, pieces, smallest, high):
    def one(position, parts):
        heights = jax.random.uniform(jax.random.fold_in(jax.random.fold_in(rng, 6), position), (parts,), jnp.float32, smallest / len(pieces), high / len(pieces))
        return jnp.repeat(jnp.exp(heights), dims[position] // parts).reshape((-1,) + (1,) * (len(dims) - position - 1))

    gain = one(*pieces[0])
    for cut in pieces[1:]:
        gain = gain * one(*cut)
    return gain


def noise(rng, shape, spread, limit, shards=(), dtype=jnp.bfloat16):
    factor_of = block_scale(rng, shape, shards, -0.22, 0.18) if shards else 1.0
    result = jax.random.normal(rng, shape, jnp.float32) * spread * factor_of
    return jnp.minimum(jnp.maximum(result, -limit), limit).astype(dtype)


def setup_inputs(seed: int = 0) -> dict:
    arg_keys = jax.random.split(jax.random.key(seed), 5)
    tokens = noise(arg_keys[0], (TOKENS, D), 1.0, 6.0, ((0, 16), (1, 16)))
    gate_weight = noise(arg_keys[1], (D, FF), D ** -0.5, 0.046875, ((0, 16), (1, 16)))
    up_weight = noise(arg_keys[2], (D, FF), D ** -0.5, 0.046875, ((0, 16), (1, 16)))
    down_weight = noise(arg_keys[3], (FF, D), FF ** -0.5, 0.0390625, ((0, 16), (1, 16)))
    return dict(tokens=tokens, gate_weight=gate_weight, up_weight=up_weight, down_weight=down_weight)


def reference(tokens, gate_weight, up_weight, down_weight):
    width = D // N_GX
    group = FF // N_GY

    def step(index, carry):
        gate_acc, up_acc = carry
        first = index.astype(jnp.int32) * width
        block = lax.dynamic_slice_in_dim(tokens, first, width, 1)
        gate_rows = lax.dynamic_slice_in_dim(gate_weight, first, width, 0)
        up_rows = lax.dynamic_slice_in_dim(up_weight, first, width, 0)
        gate_part = jnp.dot(block, gate_rows, preferred_element_type=jnp.float32).astype(jnp.bfloat16)
        up_part = jnp.dot(block, up_rows, preferred_element_type=jnp.float32).astype(jnp.bfloat16)
        gate_part, up_part = lax.optimization_barrier((gate_part, up_part))
        return (gate_acc + gate_part.astype(jnp.float32), up_acc + up_part.astype(jnp.float32))

    start = jnp.zeros((TOKENS, FF), jnp.float32)
    gate, up = lax.fori_loop(0, N_GX, step, (start, start))
    hidden = (jax.nn.silu(gate) * up).astype(jnp.bfloat16)

    def down_step(index, total):
        first = index.astype(jnp.int32) * group
        columns = lax.dynamic_slice_in_dim(hidden, first, group, 1)
        rows = lax.dynamic_slice_in_dim(down_weight, first, group, 0)
        part = jnp.dot(columns, rows, preferred_element_type=jnp.float32).astype(jnp.bfloat16)
        part = lax.optimization_barrier(part)
        return total + part.astype(jnp.float32)

    mixed = lax.fori_loop(0, N_GY, down_step, jnp.zeros((TOKENS, D), jnp.float32))
    return mixed.astype(jnp.bfloat16)
```

```python
import functools

import jax
import jax.numpy as jnp
from jax import lax
from jax.experimental import pallas as pl
from jax.experimental.pallas import tpu as pltpu
from jax.sharding import PartitionSpec as P

BF = jnp.bfloat16
F32 = jnp.float32
N = 16
FIRST = (1, 3)
SECOND = (3, 1)


def exchange(value, masks_x=(0, 0), z=0, masks_y=(0, 0), zhi=0, core=0):
    pairs = []
    for gx in range(N):
        for gy in range(N):
            other = (gx ^ (2 * masks_y[gx & 1]) ^ (8 * zhi) ^ core) * N + (gy ^ (4 * masks_x[gx & 1]) ^ z)
            pairs.append((gx * N + gy, other))
    return lax.ppermute(value, ("gx", "gy"), pairs)


def gray(v):
    return v ^ (v >> 1)


def kept(gx):
    odd = (gx & 1) == 1
    ys = [lax.select(odd, jnp.int32(gray(i)), jnp.int32(3 * gray(i) & 3)) for i in range(4)]
    return [gx ^ (2 * y) ^ (8 * z) for y in ys for z in (0, 1)]


def gathered_slot(block):
    x, z = block >> 2, block & 3
    return 8 * (z >> 1) + 2 * gray(lax.select(z < 2, x, (3 * x) & 3)) + (z & 1)


def scattered_slot(gx, block):
    x, z = block >> 2, block & 3
    return 4 * gray(lax.select((gx & 1) == 0, x, (3 * x) & 3)) + z


def pick_kernel(rows, *refs):
    *pieces, a_ref, b_ref, whole = refs
    first = 0
    for piece in pieces:
        whole[pl.ds(first, piece.shape[0]), :] = piece[...].astype(F32)
        first += piece.shape[0]
    me = lax.axis_index("gx")
    slots = [gathered_slot(block) for block in kept(me ^ 1) + kept(me)]
    for chunk, out in enumerate((a_ref, b_ref)):
        for pair in range(N // 2):
            blocks = []
            for s in slots[2 * pair : 2 * pair + 2]:
                source = pl.multiple_of(s * (2 * rows) + chunk * rows, 8)
                blocks.append(whole[pl.ds(source, rows), :])
            out[pl.ds(2 * pair * rows, 2 * rows), :] = jnp.concatenate(blocks).astype(BF)


def place_kernel(rows, *refs):
    *pieces, out_ref, whole = refs
    me = lax.axis_index("gx")
    blocks = iter(kept(me) + kept(me ^ 1))
    for piece in pieces:
        value = piece[...].astype(F32)
        for part in range(piece.shape[0] // rows):
            target = pl.multiple_of(scattered_slot(me, next(blocks)) * rows, 8)
            whole[pl.ds(target, rows), :] = value[part * rows : (part + 1) * rows]
    out_ref[...] = whole[...].astype(BF)


def pack_kernel(gate_ref, up_ref, out_ref, sems):
    copies = []
    for j in range(gate_ref.shape[1] // 128):
        for k, ref in enumerate((gate_ref, up_ref)):
            copies.append(
                pltpu.make_async_copy(
                    ref.at[:, pl.ds(128 * j, 128)], out_ref.at[:, pl.ds(256 * j + 128 * k, 128)], sems.at[2 * j + k]
                )
            )
    for copy in copies:
        copy.start()
    for copy in copies:
        copy.wait()


def pack(gate_weight, up_weight):
    width, units = gate_weight.shape
    return pl.pallas_call(
        pack_kernel,
        out_shape=jax.ShapeDtypeStruct((width, 2 * units), BF),
        in_specs=[pl.BlockSpec(memory_space=pl.ANY)] * 2,
        out_specs=pl.BlockSpec(memory_space=pltpu.VMEM),
        scratch_shapes=[pltpu.SemaphoreType.DMA((2 * units // 128,))],
        compiler_params=pltpu.CompilerParams(vmem_limit_bytes=16 * 2**20),
        cost_estimate=pl.CostEstimate(flops=0, bytes_accessed=8 * width * units, transcendentals=0),
        name="pack",
    )(gate_weight, up_weight)


def in_vmem(kernel, shapes, name, *values, scratch=(), limit=8):
    spec = pl.BlockSpec(memory_space=pltpu.VMEM)
    out = tuple(jax.ShapeDtypeStruct(shape, BF) for shape in shapes)
    result = pl.pallas_call(
        kernel,
        out_shape=out,
        in_specs=[spec] * len(values),
        out_specs=(spec,) * len(out),
        scratch_shapes=scratch,
        compiler_params=pltpu.CompilerParams(vmem_limit_bytes=limit * 2**20),
        name=name,
    )(*values)
    return result if len(out) > 1 else result[0]


def pick(pieces, rows):
    width = pieces[0].shape[1]
    return in_vmem(
        functools.partial(pick_kernel, rows),
        [(N * rows, width)] * 2,
        "pick",
        *pieces,
        scratch=[pltpu.VMEM((2 * N * rows, width), F32)],
        limit=16,
    )


def place(pieces, rows):
    shape = (N * rows, pieces[0].shape[1])
    return in_vmem(
        functools.partial(place_kernel, rows), [shape], "place", *pieces, scratch=[pltpu.VMEM(shape, F32)], limit=16
    )


def silu_kernel(a_ref, b_ref, out_ref):
    for j in range(out_ref.shape[1] // 128):
        gate = pl.ds(256 * j, 128)
        up = pl.ds(256 * j + 128, 128)
        g = a_ref[:, gate].astype(F32) + b_ref[:, gate].astype(F32)
        u = a_ref[:, up].astype(F32) + b_ref[:, up].astype(F32)
        out_ref[:, pl.ds(128 * j, 128)] = (g / (1.0 + jnp.exp(-g)) * u).astype(BF)


def silu(a, b):
    return in_vmem(silu_kernel, [(a.shape[0], a.shape[1] // 2)], "silu", a, b)


def join_kernel(*refs):
    first = 0
    for ref in refs[:-1]:
        refs[-1][pl.ds(first, ref.shape[0]), :] = ref[...]
        first += ref.shape[0]


def join(*values):
    return in_vmem(join_kernel, [(sum(v.shape[0] for v in values), values[0].shape[1])], "join", *values)


def add(a, b):
    return (a.astype(F32) + b.astype(F32)).astype(BF)


def dot(a, b):
    return jnp.dot(a, b, preferred_element_type=F32).astype(BF)


def tie(*values):
    return lax.optimization_barrier(values)


def gather_tokens(t, weight):
    t1, t2, t3 = (exchange(t, z=m) for m in (1, 2, 3))
    t1, t2, t3, weight = tie(t1, t2, t3, weight)
    h0, h1 = join(t, t1), join(t2, t3)
    p0, p1 = exchange(h0, masks_x=(1, 1)), exchange(h1, masks_x=(3, 3))
    q0, q1 = exchange(join(h0, p0), masks_x=(3, 3)), exchange(join(h1, p1), masks_x=(1, 1))
    return [h0, p0, q0, h1, p1, q1], weight


def chain(rows, down_weight):
    def halve(size, **how):
        def step(stays, got):
            v = add(stays, got)
            return v[: size * rows], v[size * rows :], how

        return step

    def first_hidden(stays, got):
        h = silu(stays, got)
        return h, h, dict(zhi=1)

    def double(**how):
        def step(stays, got):
            h = join(stays, got)
            return h, h, how

        return step

    def product(stays, got):
        s = dot(place([stays, got], rows), down_weight)
        return s[: 8 * rows], s[8 * rows :], dict(masks_x=SECOND)

    return [
        halve(4, masks_y=FIRST),
        halve(2, masks_y=SECOND),
        halve(1, zhi=1),
        first_hidden,
        double(masks_y=SECOND),
        double(masks_y=FIRST),
        double(core=1),
        product,
        halve(4, masks_x=FIRST),
    ]


def shards(tokens, gate_weight, up_weight, down_weight):
    rows = tokens.shape[0] // 2
    pieces, weight = gather_tokens(tokens, pack(gate_weight, up_weight))
    stays, got, sent = [None, None], [None, None], None
    for c, picked in enumerate(pick(pieces, rows)):
        s = dot(picked, weight)
        stays[c], sent = s[8 * rows :], s[: 8 * rows]
        got[c] = exchange(sent, core=1)
    for step in chain(rows, down_weight):
        for c in range(2):
            got[c], _ = tie(got[c], sent)
            stays[c], sent, how = step(stays[c], got[c])
            got[c] = exchange(sent, **how)
    mixed = []
    for c in range(2):
        v = add(stays[c], got[c])
        parts = [v[:rows]] + [exchange(v[m * rows : (m + 1) * rows], z=m) for m in (1, 2, 3)]
        mixed.append(functools.reduce(jnp.add, [p.astype(F32) for p in parts]).astype(BF))
    return jnp.concatenate(mixed)


def solution(mesh):
    in_specs = (P("gy", "gx"), P("gx", "gy"), P("gx", "gy"), P("gy", "gx"))
    out_specs = P("gy", "gx")
    return jax.shard_map(shards, mesh=mesh, in_specs=in_specs, out_specs=out_specs, check_vma=False)
```

```python
import functools

import jax
import jax.numpy as jnp
from jax import lax
from jax.experimental import pallas as pl
from jax.experimental.pallas import tpu as pltpu
from jax.sharding import PartitionSpec as P

BF = jnp.bfloat16
F32 = jnp.float32
N = 16
CHUNKS = 3
FIRST = (1, 3)
SECOND = (3, 1)


def exchange(value, masks_x=(0, 0), z=0, masks_y=(0, 0), zhi=0, core=0):
    pairs = []
    for gx in range(N):
        for gy in range(N):
            other = (gx ^ (2 * masks_y[gx & 1]) ^ (8 * zhi) ^ core) * N + (gy ^ (4 * masks_x[gx & 1]) ^ z)
            pairs.append((gx * N + gy, other))
    return lax.ppermute(value, ("gx", "gy"), pairs)


def gray(v):
    return v ^ (v >> 1)


def kept(gx):
    odd = (gx & 1) == 1
    ys = [lax.select(odd, jnp.int32(gray(i)), jnp.int32(3 * gray(i) & 3)) for i in range(4)]
    return [[gx ^ (2 * y) ^ (8 * z) for z in (0, 1)] for y in ys]


def x_place(gx, block):
    return gray(lax.select((gx & 1) == 0, block >> 2, (3 * (block >> 2)) & 3))


def gathered_slot(gx, block):
    return 8 * ((block >> 1) & 1) + 2 * x_place(gx, block) + (block & 1)


def scattered_slot(gx, block):
    return 4 * x_place(gx, block) + (block & 3)


def pick_kernel(rows, n, *refs):
    pieces, outs, whole = refs[: -n - 1], refs[-n - 1 : -1], refs[-1]
    first = 0
    for piece in pieces:
        whole[pl.ds(first, piece.shape[0]), :] = piece[...]
        first += piece.shape[0]
    me = lax.axis_index("gx")
    slots = [gathered_slot(me, block) for gx in (me ^ 1, me) for blocks in kept(gx) for block in blocks]
    for chunk, out in enumerate(outs):
        for k, slot in enumerate(slots):
            source = pl.multiple_of((slot * n + chunk) * rows, 16)
            out[pl.ds(k * rows, rows), :] = whole[pl.ds(source, rows), :]


def place_kernel(rows, *refs):
    *pieces, out_ref = refs
    me = lax.axis_index("gx")
    for piece, (gx, z) in zip(pieces, [(me, 0), (me, 1), (me ^ 1, 0), (me ^ 1, 1)]):
        for part, blocks in enumerate(kept(gx)):
            target = pl.multiple_of(scattered_slot(me, blocks[z]) * rows, 16)
            out_ref[pl.ds(target, rows), :] = piece[pl.ds(part * rows, rows), :]


def pack_kernel(gate_ref, up_ref, out_ref, sems):
    copies = []
    for j in range(gate_ref.shape[1] // 128):
        for k, ref in enumerate((gate_ref, up_ref)):
            copies.append(
                pltpu.make_async_copy(
                    ref.at[:, pl.ds(128 * j, 128)], out_ref.at[:, pl.ds(256 * j + 128 * k, 128)], sems.at[2 * j + k]
                )
            )
    for copy in copies:
        copy.start()
    for copy in copies:
        copy.wait()


def pack(gate_weight, up_weight):
    width, units = gate_weight.shape
    return pl.pallas_call(
        pack_kernel,
        out_shape=jax.ShapeDtypeStruct((width, 2 * units), BF),
        in_specs=[pl.BlockSpec(memory_space=pl.ANY)] * 2,
        out_specs=pl.BlockSpec(memory_space=pltpu.VMEM),
        scratch_shapes=[pltpu.SemaphoreType.DMA((2 * units // 128,))],
        compiler_params=pltpu.CompilerParams(vmem_limit_bytes=16 * 2**20),
        cost_estimate=pl.CostEstimate(flops=0, bytes_accessed=8 * width * units, transcendentals=0),
        name="pack",
    )(gate_weight, up_weight)


def in_vmem(kernel, shapes, name, *values, scratch=(), limit=8):
    spec = pl.BlockSpec(memory_space=pltpu.VMEM)
    out = tuple(jax.ShapeDtypeStruct(shape, BF) for shape in shapes)
    result = pl.pallas_call(
        kernel,
        out_shape=out,
        in_specs=[spec] * len(values),
        out_specs=(spec,) * len(out),
        scratch_shapes=scratch,
        compiler_params=pltpu.CompilerParams(vmem_limit_bytes=limit * 2**20),
        name=name,
    )(*values)
    return result if len(out) > 1 else result[0]


def pick(pieces, rows):
    width = pieces[0].shape[1]
    return in_vmem(
        functools.partial(pick_kernel, rows, CHUNKS),
        [(N * rows, width)] * CHUNKS,
        "pick",
        *pieces,
        scratch=[pltpu.VMEM((CHUNKS * N * rows, width), BF)],
        limit=16,
    )


def place(pieces, rows):
    shape = (N * rows, pieces[0].shape[1])
    return in_vmem(functools.partial(place_kernel, rows), [shape], "place", *pieces)


def silu_kernel(a_ref, b_ref, out_ref):
    for j in range(out_ref.shape[1] // 128):
        gate = pl.ds(256 * j, 128)
        up = pl.ds(256 * j + 128, 128)
        g = a_ref[:, gate].astype(F32) + b_ref[:, gate].astype(F32)
        u = a_ref[:, up].astype(F32) + b_ref[:, up].astype(F32)
        out_ref[:, pl.ds(128 * j, 128)] = (g / (1.0 + jnp.exp(-g)) * u).astype(BF)


def silu(a, b):
    return in_vmem(silu_kernel, [(a.shape[0], a.shape[1] // 2)], "silu", a, b)


def join_kernel(*refs):
    first = 0
    for ref in refs[:-1]:
        refs[-1][pl.ds(first, ref.shape[0]), :] = ref[...]
        first += ref.shape[0]


def join(*values):
    return in_vmem(join_kernel, [(sum(v.shape[0] for v in values), values[0].shape[1])], "join", *values)


def add(a, b):
    return (a.astype(F32) + b.astype(F32)).astype(BF)


def dot(a, b):
    return jnp.dot(a, b, preferred_element_type=F32).astype(BF)


def tie(*values):
    return lax.optimization_barrier(values)


def gather_tokens(t, gate_weight, up_weight):
    t1, t2, t3 = (exchange(t, z=m) for m in (1, 2, 3))
    first = join(t, t1)
    gate_weight, _ = tie(gate_weight, first)
    weight = pack(gate_weight, up_weight)
    t3, weight = tie(t3, weight)
    pieces = []
    for h in first, join(t2, t3):
        p = exchange(h, masks_x=FIRST)
        pieces += [h, p, exchange(join(h, p), masks_x=SECOND)]
    return pieces, weight


def halve(stays, got, size):
    v = add(stays, got)
    return v[:size], v[size:]


def scatter_hidden(chunks, weight, rows):
    stays, got, sent = [None] * CHUNKS, [None] * CHUNKS, None
    for c, picked in enumerate(chunks):
        s = dot(picked, weight)
        stays[c], sent = s[8 * rows :], s[: 8 * rows]
        got[c] = exchange(sent, core=1)
    for size, how in (4, dict(masks_y=FIRST)), (2, dict(masks_y=SECOND)), (1, dict(zhi=1)):
        for c in range(CHUNKS):
            got[c], _ = tie(got[c], sent)
            stays[c], sent = halve(stays[c], got[c], size * rows)
            got[c] = exchange(sent, **how)
    hidden = [silu(stays[0], got[0])]
    for c in range(1, CHUNKS):
        got[c], _ = tie(got[c], hidden[-1])
        hidden.append(silu(stays[c], got[c]))
    return hidden


def gather_hidden(hidden):
    half = [exchange(h, zhi=1) for h in hidden]
    halves = []
    for h in join(*hidden), None:
        if h is None:
            h = join(*half)
        h = join(h, exchange(h, masks_y=SECOND))
        halves.append(join(h, exchange(h, masks_y=FIRST)))
    return halves + [exchange(h, core=1) for h in halves]


def scatter_out(hidden, weight, rows):
    width = weight.shape[1] // 2
    stays, got = [None, None], [None, None]
    for c in range(2):
        s = dot(hidden, weight[:, c * width : (c + 1) * width])
        stays[c], sent = s[: 8 * rows], s[8 * rows :]
        got[c] = exchange(sent, masks_x=SECOND)
    got[0], _ = tie(got[0], sent)
    for c in range(2):
        if c == 1:
            got[1], got[0] = tie(got[1], got[0])
        stays[c], sent = halve(stays[c], got[c], 4 * rows)
        got[c] = exchange(sent, masks_x=FIRST)
    columns = []
    for c in range(2):
        v = add(stays[c], got[c])
        parts = [v[:rows]] + [exchange(v[m * rows : (m + 1) * rows], z=m) for m in (1, 2, 3)]
        columns.append(functools.reduce(jnp.add, [p.astype(F32) for p in parts]).astype(BF))
    return jnp.concatenate(columns, axis=1)


def shards(tokens, gate_weight, up_weight, down_weight):
    rows = tokens.shape[0]
    pieces, weight = gather_tokens(tokens, gate_weight, up_weight)
    hidden = scatter_hidden(pick(pieces, rows // CHUNKS), weight, rows // CHUNKS)
    return scatter_out(place(gather_hidden(hidden), rows), down_weight, rows)


def solution(mesh):
    in_specs = (P("gy", "gx"), P("gx", "gy"), P("gx", "gy"), P("gy", "gx"))
    out_specs = P("gy", "gx")
    return jax.shard_map(shards, mesh=mesh, in_specs=in_specs, out_specs=out_specs, check_vma=False)
```

```python
import functools

import jax
import jax.numpy as jnp
from jax import lax
from jax.experimental import pallas as pl
from jax.experimental.pallas import tpu as pltpu
from jax.sharding import PartitionSpec as P

BF = jnp.bfloat16
F32 = jnp.float32
N = 16
CHUNKS = 3
TURNS = [(0, 0), (1, 0), (0, 1), (2, 0), (1, 1), (2, 1), (0, 2), (1, 2)]
TURNS += [(0, 3), (2, 2), (1, 3), (0, 4), (2, 3), (1, 4), (2, 4)]
FIRST = (1, 3)
SECOND = (3, 1)


def exchange(value, masks_x=(0, 0), z=0, masks_y=(0, 0), zhi=0, core=0):
    pairs = []
    for gx in range(N):
        for gy in range(N):
            other = (gx ^ (2 * masks_y[gx & 1]) ^ (8 * zhi) ^ core) * N + (gy ^ (4 * masks_x[gx & 1]) ^ z)
            pairs.append((gx * N + gy, other))
    return lax.ppermute(value, ("gx", "gy"), pairs)


def gray(v):
    return v ^ (v >> 1)


def kept(gx):
    odd = (gx & 1) == 1
    ys = [lax.select(odd, jnp.int32(gray(i)), jnp.int32(3 * gray(i) & 3)) for i in range(4)]
    return [[gx ^ (2 * y) ^ (8 * z) for z in (0, 1)] for y in ys]


def x_place(gx, block):
    return gray(lax.select((gx & 1) == 0, block >> 2, (3 * (block >> 2)) & 3))


def gathered_slot(gx, block):
    return 8 * ((block >> 1) & 1) + 2 * x_place(gx, block) + (block & 1)


def scattered_slot(gx, block):
    return 4 * x_place(gx, block) + (block & 3)


def pick_kernel(rows, n, *refs):
    pieces, outs, whole = refs[: -n - 1], refs[-n - 1 : -1], refs[-1]
    first = 0
    for piece in pieces:
        whole[pl.ds(first, piece.shape[0]), :] = piece[...]
        first += piece.shape[0]
    me = lax.axis_index("gx")
    slots = [gathered_slot(me, block) for gx in (me ^ 1, me) for blocks in kept(gx) for block in blocks]
    for chunk, out in enumerate(outs):
        for k, slot in enumerate(slots):
            source = pl.multiple_of((slot * n + chunk) * rows, 16)
            out[pl.ds(k * rows, rows), :] = whole[pl.ds(source, rows), :]


def place_kernel(rows, *refs):
    *pieces, out_ref = refs
    me = lax.axis_index("gx")
    for piece, (gx, z) in zip(pieces, [(me, 0), (me, 1), (me ^ 1, 0), (me ^ 1, 1)]):
        for part, blocks in enumerate(kept(gx)):
            target = pl.multiple_of(scattered_slot(me, blocks[z]) * rows, 16)
            out_ref[pl.ds(target, rows), :] = piece[pl.ds(part * rows, rows), :]


def pack_kernel(gate_ref, up_ref, out_ref, sems):
    copies = []
    for j in range(gate_ref.shape[1] // 128):
        for k, ref in enumerate((gate_ref, up_ref)):
            copies.append(
                pltpu.make_async_copy(
                    ref.at[:, pl.ds(128 * j, 128)], out_ref.at[:, pl.ds(256 * j + 128 * k, 128)], sems.at[2 * j + k]
                )
            )
    for copy in copies:
        copy.start()
    for copy in copies:
        copy.wait()


def pack(gate_weight, up_weight):
    width, units = gate_weight.shape
    return pl.pallas_call(
        pack_kernel,
        out_shape=jax.ShapeDtypeStruct((width, 2 * units), BF),
        in_specs=[pl.BlockSpec(memory_space=pl.ANY)] * 2,
        out_specs=pl.BlockSpec(memory_space=pltpu.VMEM),
        scratch_shapes=[pltpu.SemaphoreType.DMA((2 * units // 128,))],
        compiler_params=pltpu.CompilerParams(vmem_limit_bytes=16 * 2**20),
        cost_estimate=pl.CostEstimate(flops=0, bytes_accessed=8 * width * units, transcendentals=0),
        name="pack",
    )(gate_weight, up_weight)


def in_vmem(kernel, shapes, name, *values, scratch=(), limit=8):
    spec = pl.BlockSpec(memory_space=pltpu.VMEM)
    out = tuple(jax.ShapeDtypeStruct(shape, BF) for shape in shapes)
    result = pl.pallas_call(
        kernel,
        out_shape=out,
        in_specs=[spec] * len(values),
        out_specs=(spec,) * len(out),
        scratch_shapes=scratch,
        compiler_params=pltpu.CompilerParams(vmem_limit_bytes=limit * 2**20),
        name=name,
    )(*values)
    return result if len(out) > 1 else result[0]


def pick(pieces, rows):
    width = pieces[0].shape[1]
    return in_vmem(
        functools.partial(pick_kernel, rows, CHUNKS),
        [(N * rows, width)] * CHUNKS,
        "pick",
        *pieces,
        scratch=[pltpu.VMEM((CHUNKS * N * rows, width), BF)],
        limit=16,
    )


def place(pieces, rows):
    shape = (N * rows, pieces[0].shape[1])
    return in_vmem(functools.partial(place_kernel, rows), [shape], "place", *pieces)


def silu_kernel(a_ref, b_ref, out_ref):
    for j in range(out_ref.shape[1] // 128):
        gate = pl.ds(256 * j, 128)
        up = pl.ds(256 * j + 128, 128)
        g = a_ref[:, gate].astype(F32) + b_ref[:, gate].astype(F32)
        u = a_ref[:, up].astype(F32) + b_ref[:, up].astype(F32)
        out_ref[:, pl.ds(128 * j, 128)] = (g / (1.0 + jnp.exp(-g)) * u).astype(BF)


def silu(a, b):
    return in_vmem(silu_kernel, [(a.shape[0], a.shape[1] // 2)], "silu", a, b)


def join_kernel(*refs):
    first = 0
    for ref in refs[:-1]:
        refs[-1][pl.ds(first, ref.shape[0]), :] = ref[...]
        first += ref.shape[0]


def join(*values):
    return in_vmem(join_kernel, [(sum(v.shape[0] for v in values), values[0].shape[1])], "join", *values)


def add(a, b):
    return (a.astype(F32) + b.astype(F32)).astype(BF)


def dot(a, b):
    return jnp.dot(a, b, preferred_element_type=F32).astype(BF)


def tie(*values):
    return lax.optimization_barrier(values)


def gather_tokens(t, gate_weight, up_weight):
    t1, t2, t3 = (exchange(t, z=m) for m in (1, 2, 3))
    pieces = []
    for h in join(t, t1), join(t2, t3):
        p = exchange(h, masks_x=FIRST)
        both = join(h, p)
        pieces += [h, p, exchange(both, masks_x=SECOND)]
    gate_weight, _ = tie(gate_weight, both)
    return pieces, pack(gate_weight, up_weight)


def halve(stays, got, size):
    v = add(stays, got)
    return v[:size], v[size:]


def scatter_hidden(chunks, weight, rows):
    stays, got = [None] * CHUNKS, [None] * CHUNKS

    def step(c, k, turn):
        if k == 0:
            picked = chunks[c] if turn is None else tie(chunks[c], turn)[0]
            s = dot(picked, weight)
            stays[c], sent, how = s[8 * rows :], s[: 8 * rows], dict(core=1)
        else:
            got[c], _ = tie(got[c], turn)
            if k == 4:
                stays[c] = sent = silu(stays[c], got[c])
                how = dict(zhi=1)
            else:
                size, how = [(4, dict(masks_y=FIRST)), (2, dict(masks_y=SECOND)), (1, dict(zhi=1))][k - 1]
                stays[c], sent = halve(stays[c], got[c], size * rows)
        got[c] = exchange(sent, **how)
        return sent

    turn = None
    for c, k in TURNS:
        turn = step(c, k, turn)
    return stays, got


def gather_hidden(own, other):
    halves = []
    for hidden in own, other:
        h = join(*hidden)
        h = join(h, exchange(h, masks_y=SECOND))
        halves.append(join(h, exchange(h, masks_y=FIRST)))
    return halves + [exchange(h, core=1) for h in halves]


def scatter_out(hidden, weight, rows):
    width = weight.shape[1] // 2
    stays, got = [None, None], [None, None]
    for c in range(2):
        s = dot(hidden, weight[:, c * width : (c + 1) * width])
        stays[c], sent = s[: 8 * rows], s[8 * rows :]
        got[c] = exchange(sent, masks_x=SECOND)
    got[0], _ = tie(got[0], sent)
    for c in range(2):
        if c == 1:
            got[1], got[0] = tie(got[1], got[0])
        stays[c], sent = halve(stays[c], got[c], 4 * rows)
        got[c] = exchange(sent, masks_x=FIRST)
    columns = []
    for c in range(2):
        v = add(stays[c], got[c])
        parts = [v[:rows]] + [exchange(v[m * rows : (m + 1) * rows], z=m) for m in (1, 2, 3)]
        columns.append(functools.reduce(jnp.add, [p.astype(F32) for p in parts]).astype(BF))
    return jnp.concatenate(columns, axis=1)


def shards(tokens, gate_weight, up_weight, down_weight):
    rows = tokens.shape[0]
    pieces, weight = gather_tokens(tokens, gate_weight, up_weight)
    hidden = scatter_hidden(pick(pieces, rows // CHUNKS), weight, rows // CHUNKS)
    return scatter_out(place(gather_hidden(*hidden), rows), down_weight, rows)


def solution(mesh):
    in_specs = (P("gy", "gx"), P("gx", "gy"), P("gx", "gy"), P("gy", "gx"))
    out_specs = P("gy", "gx")
    return jax.shard_map(shards, mesh=mesh, in_specs=in_specs, out_specs=out_specs, check_vma=False)
```

```python
import functools

import jax
import jax.numpy as jnp
from jax import lax
from jax.experimental import pallas as pl
from jax.experimental.pallas import tpu as pltpu
from jax.sharding import PartitionSpec as P

BF = jnp.bfloat16
F32 = jnp.float32
N = 16
CHUNKS = 3
FIRST = (1, 3)
SECOND = (3, 1)


def exchange(value, masks_x=(0, 0), z=0, masks_y=(0, 0), zhi=0, core=0):
    pairs = []
    for gx in range(N):
        for gy in range(N):
            other = (gx ^ (2 * masks_y[gx & 1]) ^ (8 * zhi) ^ core) * N + (gy ^ (4 * masks_x[gx & 1]) ^ z)
            pairs.append((gx * N + gy, other))
    return lax.ppermute(value, ("gx", "gy"), pairs)


def gray(v):
    return v ^ (v >> 1)


def kept(gx):
    odd = (gx & 1) == 1
    ys = [lax.select(odd, jnp.int32(gray(i)), jnp.int32(3 * gray(i) & 3)) for i in range(4)]
    return [[gx ^ (2 * y) ^ (8 * z) for z in (0, 1)] for y in ys]


def x_place(gx, block):
    return gray(lax.select((gx & 1) == 0, block >> 2, (3 * (block >> 2)) & 3))


def gathered_slot(gx, block):
    return 8 * ((block >> 1) & 1) + 2 * x_place(gx, block) + (block & 1)


def scattered_slot(gx, block):
    return 4 * x_place(gx, block) + (block & 3)


def pick_kernel(rows, n, *refs):
    pieces, outs, whole = refs[: -n - 1], refs[-n - 1 : -1], refs[-1]
    first = 0
    for piece in pieces:
        whole[pl.ds(first, piece.shape[0]), :] = piece[...]
        first += piece.shape[0]
    me = lax.axis_index("gx")
    slots = [gathered_slot(me, block) for gx in (me ^ 1, me) for blocks in kept(gx) for block in blocks]
    for chunk, out in enumerate(outs):
        for k, slot in enumerate(slots):
            source = pl.multiple_of((slot * n + chunk) * rows, 16)
            out[pl.ds(k * rows, rows), :] = whole[pl.ds(source, rows), :]


def place_kernel(rows, segments, *refs):
    *pieces, out_ref = refs
    me = lax.axis_index("gx")
    for piece, core, z, stride, offset in segments:
        for part, blocks in enumerate(kept(me ^ core)):
            target = pl.multiple_of(scattered_slot(me, blocks[z]) * rows, 16)
            out_ref[pl.ds(target, rows), :] = pieces[piece][pl.ds(part * stride + offset, rows), :]


def pack_kernel(gate_ref, up_ref, out_ref, sems):
    copies = []
    for j in range(gate_ref.shape[1] // 128):
        for k, ref in enumerate((gate_ref, up_ref)):
            copies.append(
                pltpu.make_async_copy(
                    ref.at[:, pl.ds(128 * j, 128)], out_ref.at[:, pl.ds(256 * j + 128 * k, 128)], sems.at[2 * j + k]
                )
            )
    for copy in copies:
        copy.start()
    for copy in copies:
        copy.wait()


def pack(gate_weight, up_weight):
    width, units = gate_weight.shape
    return pl.pallas_call(
        pack_kernel,
        out_shape=jax.ShapeDtypeStruct((width, 2 * units), BF),
        in_specs=[pl.BlockSpec(memory_space=pl.ANY)] * 2,
        out_specs=pl.BlockSpec(memory_space=pltpu.VMEM),
        scratch_shapes=[pltpu.SemaphoreType.DMA((2 * units // 128,))],
        compiler_params=pltpu.CompilerParams(vmem_limit_bytes=16 * 2**20),
        cost_estimate=pl.CostEstimate(flops=0, bytes_accessed=8 * width * units, transcendentals=0),
        name="pack",
    )(gate_weight, up_weight)


def in_vmem(kernel, shapes, name, *values, scratch=(), limit=8):
    spec = pl.BlockSpec(memory_space=pltpu.VMEM)
    out = tuple(jax.ShapeDtypeStruct(shape, BF) for shape in shapes)
    result = pl.pallas_call(
        kernel,
        out_shape=out,
        in_specs=[spec] * len(values),
        out_specs=(spec,) * len(out),
        scratch_shapes=scratch,
        compiler_params=pltpu.CompilerParams(vmem_limit_bytes=limit * 2**20),
        name=name,
    )(*values)
    return result if len(out) > 1 else result[0]


def pick(pieces, rows):
    width = pieces[0].shape[1]
    return in_vmem(
        functools.partial(pick_kernel, rows, CHUNKS),
        [(N * rows, width)] * CHUNKS,
        "pick",
        *pieces,
        scratch=[pltpu.VMEM((CHUNKS * N * rows, width), BF)],
        limit=16,
    )


def place(pieces, rows, segments):
    shape = (N * rows, pieces[0].shape[1])
    return in_vmem(functools.partial(place_kernel, rows, segments), [shape], "place", *pieces)


def silu_kernel(a_ref, b_ref, out_ref):
    for j in range(out_ref.shape[1] // 128):
        gate = pl.ds(256 * j, 128)
        up = pl.ds(256 * j + 128, 128)
        g = a_ref[:, gate].astype(F32) + b_ref[:, gate].astype(F32)
        u = a_ref[:, up].astype(F32) + b_ref[:, up].astype(F32)
        out_ref[:, pl.ds(128 * j, 128)] = (g / (1.0 + jnp.exp(-g)) * u).astype(BF)


def silu(a, b):
    return in_vmem(silu_kernel, [(a.shape[0], a.shape[1] // 2)], "silu", a, b)


def join_kernel(*refs):
    first = 0
    for ref in refs[:-1]:
        refs[-1][pl.ds(first, ref.shape[0]), :] = ref[...]
        first += ref.shape[0]


def join(*values):
    return in_vmem(join_kernel, [(sum(v.shape[0] for v in values), values[0].shape[1])], "join", *values)


def add(a, b):
    return (a.astype(F32) + b.astype(F32)).astype(BF)


def dot(a, b):
    return jnp.dot(a, b, preferred_element_type=F32).astype(BF)


def tie(*values):
    return lax.optimization_barrier(values)


def gather_tokens(t, gate_weight, up_weight):
    t1, t2, t3 = (exchange(t, z=m) for m in (1, 2, 3))
    pieces = []
    for h in join(t, t1), join(t2, t3):
        p = exchange(h, masks_x=FIRST)
        both = join(h, p)
        pieces += [h, p, exchange(both, masks_x=SECOND)]
    gate_weight, _ = tie(gate_weight, both)
    return pieces, pack(gate_weight, up_weight)


def halve(stays, got, size):
    v = add(stays, got)
    return v[:size], v[size:]


def feed_forward(chunks, gate_up_weight, down_weight, rows):
    own, got, other, waves, turn = {}, {}, {}, {}, [None]

    def after(value):
        return value if turn[0] is None else tie(value, turn[0])[0]

    def send(value, **how):
        turn[0] = value
        return exchange(value, **how)

    def product(c):
        s = dot(after(chunks[c]), gate_up_weight)
        own[c], got[c] = s[8 * rows :], send(s[: 8 * rows], core=1)

    def sums(c, size, **how):
        own[c], sent = halve(own[c], after(got[c]), size * rows)
        got[c] = send(sent, **how)

    def y_first(c):
        sums(c, 4, masks_y=FIRST)

    def y_second(c):
        sums(c, 2, masks_y=SECOND)

    def z_hi(c):
        sums(c, 1, zhi=1)

    def hidden(c):
        own[c] = silu(own[c], after(got[c]))
        other[c] = send(own[c], zhi=1)

    def start(wave, *parts):
        h = after(parts[-1]) if len(parts) == 1 else join(*parts[:-1], after(parts[-1]))
        waves[wave] = h, send(h, masks_y=SECOND)

    def widen(wave, **how):
        h, more = waves[wave]
        h = join(h, after(more))
        waves[wave] = h, send(h, **how)

    product(0)
    product(1)
    y_first(0)
    product(2)
    y_first(1)
    y_first(2)
    y_second(0)
    y_second(1)
    z_hi(0)
    y_second(2)
    z_hi(1)
    hidden(0)
    z_hi(2)
    hidden(1)
    hidden(2)
    own[2], other[0], other[1] = tie(own[2], other[0], other[1])
    start(0, own[0], own[1], own[2], other[0], other[1])
    start(1, other[2])
    widen(0, masks_y=FIRST)
    widen(1, masks_y=FIRST)
    (h, more), (first, last) = waves[0], waves[1]
    more, last = tie(more, last)
    waves[0], waves[1] = (h, more), (first, last)
    widen(0, core=1)
    widen(1, core=1)

    groups = (2 * rows, [(0, 0, 5 * rows, 0), (0, 1, 5 * rows, 3 * rows)]), (
        rows,
        [(0, 0, 5 * rows, 2 * rows), (1, 1, rows, 0)],
    )
    stays, got, output = [], [], []
    for size, sources in groups:
        used = sorted({wave for wave, *_ in sources})
        pieces = [piece for wave in used for piece in waves[wave]]
        segments = [(2 * used.index(wave) + core, core, *where) for wave, *where in sources for core in (0, 1)]
        s = dot(place(pieces, size, segments), down_weight)
        stays.append(s[: 8 * size])
        got.append(send(s[8 * size :], masks_x=SECOND))
    for g, (size, _) in enumerate(groups):
        stays[g], sent = halve(stays[g], after(got[g]), 4 * size)
        got[g] = send(sent, masks_x=FIRST)
    for g, (size, _) in enumerate(groups):
        v = turn[0] = add(stays[g], after(got[g]))
        parts = [v[:size]] + [exchange(v[m * size : (m + 1) * size], z=m) for m in (1, 2, 3)]
        output.append(functools.reduce(jnp.add, [p.astype(F32) for p in parts]).astype(BF))
    return jnp.concatenate(output)


def shards(tokens, gate_weight, up_weight, down_weight):
    rows = tokens.shape[0] // CHUNKS
    pieces, weight = gather_tokens(tokens, gate_weight, up_weight)
    return feed_forward(pick(pieces, rows), weight, down_weight, rows)


def solution(mesh):
    in_specs = (P("gy", "gx"), P("gx", "gy"), P("gx", "gy"), P("gy", "gx"))
    out_specs = P("gy", "gx")
    return jax.shard_map(shards, mesh=mesh, in_specs=in_specs, out_specs=out_specs, check_vma=False)
```

```python
import functools

import jax
import jax.numpy as jnp
from jax import lax
from jax.experimental import pallas as pl
from jax.experimental.pallas import tpu as pltpu
from jax.sharding import PartitionSpec as P

BF = jnp.bfloat16
F32 = jnp.float32
N = 16
CHUNKS = 3
TURNS = [(0, 0), (1, 0), (0, 1), (2, 0), (1, 1), (2, 1), (0, 2), (1, 2)]
TURNS += [(0, 3), (2, 2), (1, 3), (0, 4), (2, 3), (1, 4), (2, 4)]
FIRST = (1, 3)
SECOND = (3, 1)


def exchange(value, masks_x=(0, 0), z=0, masks_y=(0, 0), zhi=0, core=0):
    pairs = []
    for gx in range(N):
        for gy in range(N):
            other = (gx ^ (2 * masks_y[gx & 1]) ^ (8 * zhi) ^ core) * N + (gy ^ (4 * masks_x[gx & 1]) ^ z)
            pairs.append((gx * N + gy, other))
    return lax.ppermute(value, ("gx", "gy"), pairs)


def gray(v):
    return v ^ (v >> 1)


def kept(gx):
    odd = (gx & 1) == 1
    ys = [lax.select(odd, jnp.int32(gray(i)), jnp.int32(3 * gray(i) & 3)) for i in range(4)]
    return [[gx ^ (2 * y) ^ (8 * z) for z in (0, 1)] for y in ys]


def x_place(gx, block):
    return gray(lax.select((gx & 1) == 0, block >> 2, (3 * (block >> 2)) & 3))


def gathered_slot(gx, block):
    return 8 * ((block >> 1) & 1) + 2 * x_place(gx, block) + (block & 1)


def scattered_slot(gx, block):
    return 4 * x_place(gx, block) + (block & 3)


def pick_kernel(rows, n, *refs):
    pieces, outs, whole = refs[: -n - 1], refs[-n - 1 : -1], refs[-1]
    first = 0
    for piece in pieces:
        whole[pl.ds(first, piece.shape[0]), :] = piece[...]
        first += piece.shape[0]
    me = lax.axis_index("gx")
    slots = [gathered_slot(me, block) for gx in (me ^ 1, me) for blocks in kept(gx) for block in blocks]
    for chunk, out in enumerate(outs):
        for k, slot in enumerate(slots):
            source = pl.multiple_of((slot * n + chunk) * rows, 16)
            out[pl.ds(k * rows, rows), :] = whole[pl.ds(source, rows), :]


def place_kernel(rows, *refs):
    *pieces, out_ref = refs
    me = lax.axis_index("gx")
    for piece, (gx, z) in zip(pieces, [(me, 0), (me, 1), (me ^ 1, 0), (me ^ 1, 1)]):
        for part, blocks in enumerate(kept(gx)):
            target = pl.multiple_of(scattered_slot(me, blocks[z]) * rows, 16)
            out_ref[pl.ds(target, rows), :] = piece[pl.ds(part * rows, rows), :]


def pack_kernel(gate_ref, up_ref, out_ref, sems):
    copies = []
    for j in range(gate_ref.shape[1] // 128):
        for k, ref in enumerate((gate_ref, up_ref)):
            copies.append(
                pltpu.make_async_copy(
                    ref.at[:, pl.ds(128 * j, 128)], out_ref.at[:, pl.ds(256 * j + 128 * k, 128)], sems.at[2 * j + k]
                )
            )
    for copy in copies:
        copy.start()
    for copy in copies:
        copy.wait()


def pack(gate_weight, up_weight):
    width, units = gate_weight.shape
    return pl.pallas_call(
        pack_kernel,
        out_shape=jax.ShapeDtypeStruct((width, 2 * units), BF),
        in_specs=[pl.BlockSpec(memory_space=pl.ANY)] * 2,
        out_specs=pl.BlockSpec(memory_space=pltpu.VMEM),
        scratch_shapes=[pltpu.SemaphoreType.DMA((2 * units // 128,))],
        compiler_params=pltpu.CompilerParams(vmem_limit_bytes=16 * 2**20),
        cost_estimate=pl.CostEstimate(flops=0, bytes_accessed=8 * width * units, transcendentals=0),
        name="pack",
    )(gate_weight, up_weight)


def in_vmem(kernel, shapes, name, *values, scratch=(), limit=8):
    spec = pl.BlockSpec(memory_space=pltpu.VMEM)
    out = tuple(jax.ShapeDtypeStruct(shape, BF) for shape in shapes)
    result = pl.pallas_call(
        kernel,
        out_shape=out,
        in_specs=[spec] * len(values),
        out_specs=(spec,) * len(out),
        scratch_shapes=scratch,
        compiler_params=pltpu.CompilerParams(vmem_limit_bytes=limit * 2**20),
        name=name,
    )(*values)
    return result if len(out) > 1 else result[0]


def pick(pieces, rows):
    width = pieces[0].shape[1]
    return in_vmem(
        functools.partial(pick_kernel, rows, CHUNKS),
        [(N * rows, width)] * CHUNKS,
        "pick",
        *pieces,
        scratch=[pltpu.VMEM((CHUNKS * N * rows, width), BF)],
        limit=16,
    )


def place(pieces, rows):
    shape = (N * rows, pieces[0].shape[1])
    return in_vmem(functools.partial(place_kernel, rows), [shape], "place", *pieces)


def silu_kernel(a_ref, b_ref, out_ref):
    for j in range(out_ref.shape[1] // 128):
        gate = pl.ds(256 * j, 128)
        up = pl.ds(256 * j + 128, 128)
        g = a_ref[:, gate].astype(F32) + b_ref[:, gate].astype(F32)
        u = a_ref[:, up].astype(F32) + b_ref[:, up].astype(F32)
        out_ref[:, pl.ds(128 * j, 128)] = (g / (1.0 + jnp.exp(-g)) * u).astype(BF)


def silu(a, b):
    return in_vmem(silu_kernel, [(a.shape[0], a.shape[1] // 2)], "silu", a, b)


def join_kernel(*refs):
    first = 0
    for ref in refs[:-1]:
        refs[-1][pl.ds(first, ref.shape[0]), :] = ref[...]
        first += ref.shape[0]


def join(*values):
    return in_vmem(join_kernel, [(sum(v.shape[0] for v in values), values[0].shape[1])], "join", *values)


def add(a, b):
    return (a.astype(F32) + b.astype(F32)).astype(BF)


def dot(a, b):
    return jnp.dot(a, b, preferred_element_type=F32).astype(BF)


def tie(*values):
    return lax.optimization_barrier(values)


def gather_tokens(t, gate_weight, up_weight):
    t1, t2, t3 = (exchange(t, z=m) for m in (1, 2, 3))
    pieces = []
    for h in join(t, t1), join(t2, t3):
        p = exchange(h, masks_x=FIRST)
        both = join(h, p)
        pieces += [h, p, exchange(both, masks_x=SECOND)]
    gate_weight, _ = tie(gate_weight, both)
    return pieces, pack(gate_weight, up_weight)


def halve(stays, got, size):
    v = add(stays, got)
    return v[:size], v[size:]


def scatter_hidden(chunks, weight, rows):
    stays, got = [None] * CHUNKS, [None] * CHUNKS

    def step(c, k, turn):
        if k == 0:
            picked = chunks[c] if turn is None else tie(chunks[c], turn)[0]
            s = dot(picked, weight)
            stays[c], sent, how = s[8 * rows :], s[: 8 * rows], dict(core=1)
        else:
            got[c], _ = tie(got[c], turn)
            if k == 4:
                stays[c] = sent = silu(stays[c], got[c])
                how = dict(zhi=1)
            else:
                size, how = [(4, dict(masks_y=FIRST)), (2, dict(masks_y=SECOND)), (1, dict(zhi=1))][k - 1]
                stays[c], sent = halve(stays[c], got[c], size * rows)
        got[c] = exchange(sent, **how)
        return sent

    turn = None
    for c, k in TURNS:
        turn = step(c, k, turn)
    return stays, got


def gather_hidden(own, other):
    halves = []
    for hidden in own, other:
        h = join(*hidden)
        h = join(h, exchange(h, masks_y=SECOND))
        halves.append(join(h, exchange(h, masks_y=FIRST)))
    return halves + [exchange(h, core=1) for h in halves]


def scatter_out(hidden, weight, rows):
    parts, stays, got = (slice(0, 640), slice(640, None)), [None, None], [None, None]
    for c, part in enumerate(parts):
        s = dot(hidden, weight[:, part])
        stays[c], turn = s[: 8 * rows], s[8 * rows :]
        got[c] = exchange(turn, masks_x=SECOND)
    for c in range(2):
        got[c], _ = tie(got[c], turn)
        stays[c], turn = halve(stays[c], got[c], 4 * rows)
        got[c] = exchange(turn, masks_x=FIRST)
    columns = []
    for c in range(2):
        if c == 1:
            got[1], z[1] = tie(got[1], z[1])
        v = add(stays[c], got[c])
        z = [v[:rows]] + [exchange(v[m * rows : (m + 1) * rows], z=m) for m in (1, 2, 3)]
        columns.append(z)
    columns = [functools.reduce(jnp.add, [p.astype(F32) for p in z]).astype(BF) for z in columns]
    return jnp.concatenate(columns, axis=1)


def shards(tokens, gate_weight, up_weight, down_weight):
    rows = tokens.shape[0]
    pieces, weight = gather_tokens(tokens, gate_weight, up_weight)
    hidden = scatter_hidden(pick(pieces, rows // CHUNKS), weight, rows // CHUNKS)
    return scatter_out(place(gather_hidden(*hidden), rows), down_weight, rows)


def solution(mesh):
    in_specs = (P("gy", "gx"), P("gx", "gy"), P("gx", "gy"), P("gy", "gx"))
    out_specs = P("gy", "gx")
    return jax.shard_map(shards, mesh=mesh, in_specs=in_specs, out_specs=out_specs, check_vma=False)
```

```python
import functools

import jax
import jax.numpy as jnp
from jax import lax
from jax.experimental import pallas as pl
from jax.experimental.pallas import tpu as pltpu
from jax.sharding import PartitionSpec as P

BF = jnp.bfloat16
F32 = jnp.float32
N = 16
CHUNKS = 3
TURNS = [(0, 0), (1, 0), (0, 1), (2, 0), (1, 1), (0, 2), (2, 1), (0, 3)]
TURNS += [(1, 2), (2, 2), (1, 3), (0, 4), (2, 3), (1, 4), (2, 4)]
FIRST = (1, 3)
SECOND = (3, 1)


def exchange(value, masks_x=(0, 0), z=0, masks_y=(0, 0), zhi=0, core=0):
    pairs = []
    for gx in range(N):
        for gy in range(N):
            other = (gx ^ (2 * masks_y[gx & 1]) ^ (8 * zhi) ^ core) * N + (gy ^ (4 * masks_x[gx & 1]) ^ z)
            pairs.append((gx * N + gy, other))
    return lax.ppermute(value, ("gx", "gy"), pairs)


def gray(v):
    return v ^ (v >> 1)


def kept(gx):
    odd = (gx & 1) == 1
    ys = [lax.select(odd, jnp.int32(gray(i)), jnp.int32(3 * gray(i) & 3)) for i in range(4)]
    return [[gx ^ (2 * y) ^ (8 * z) for z in (0, 1)] for y in ys]


def x_place(gx, block):
    return gray(lax.select((gx & 1) == 0, block >> 2, (3 * (block >> 2)) & 3))


def gathered_slot(gx, block):
    return 8 * ((block >> 1) & 1) + 2 * x_place(gx, block) + (block & 1)


def scattered_slot(gx, block):
    return 4 * x_place(gx, block) + (block & 3)


def pick_kernel(rows, n, *refs):
    pieces, outs, whole = refs[: -n - 1], refs[-n - 1 : -1], refs[-1]
    first = 0
    for piece in pieces:
        whole[pl.ds(first, piece.shape[0]), :] = piece[...]
        first += piece.shape[0]
    me = lax.axis_index("gx")
    slots = [gathered_slot(me, block) for gx in (me ^ 1, me) for blocks in kept(gx) for block in blocks]
    for chunk, out in enumerate(outs):
        for k, slot in enumerate(slots):
            source = pl.multiple_of((slot * n + chunk) * rows, 16)
            out[pl.ds(k * rows, rows), :] = whole[pl.ds(source, rows), :]


def place_kernel(rows, *refs):
    *pieces, out_ref = refs
    me = lax.axis_index("gx")
    for piece, (gx, z) in zip(pieces, [(me, 0), (me, 1), (me ^ 1, 0), (me ^ 1, 1)]):
        for part, blocks in enumerate(kept(gx)):
            target = pl.multiple_of(scattered_slot(me, blocks[z]) * rows, 16)
            out_ref[pl.ds(target, rows), :] = piece[pl.ds(part * rows, rows), :]


def pack_kernel(gate_ref, up_ref, out_ref, sems):
    copies = []
    for j in range(gate_ref.shape[1] // 128):
        for k, ref in enumerate((gate_ref, up_ref)):
            copies.append(
                pltpu.make_async_copy(
                    ref.at[:, pl.ds(128 * j, 128)], out_ref.at[:, pl.ds(256 * j + 128 * k, 128)], sems.at[2 * j + k]
                )
            )
    for copy in copies:
        copy.start()
    for copy in copies:
        copy.wait()


def pack(gate_weight, up_weight):
    width, units = gate_weight.shape
    return pl.pallas_call(
        pack_kernel,
        out_shape=jax.ShapeDtypeStruct((width, 2 * units), BF),
        in_specs=[pl.BlockSpec(memory_space=pl.ANY)] * 2,
        out_specs=pl.BlockSpec(memory_space=pltpu.VMEM),
        scratch_shapes=[pltpu.SemaphoreType.DMA((2 * units // 128,))],
        compiler_params=pltpu.CompilerParams(vmem_limit_bytes=16 * 2**20),
        cost_estimate=pl.CostEstimate(flops=0, bytes_accessed=8 * width * units, transcendentals=0),
        name="pack",
    )(gate_weight, up_weight)


def in_vmem(kernel, shapes, name, *values, scratch=(), limit=8):
    spec = pl.BlockSpec(memory_space=pltpu.VMEM)
    out = tuple(jax.ShapeDtypeStruct(shape, BF) for shape in shapes)
    result = pl.pallas_call(
        kernel,
        out_shape=out,
        in_specs=[spec] * len(values),
        out_specs=(spec,) * len(out),
        scratch_shapes=scratch,
        compiler_params=pltpu.CompilerParams(vmem_limit_bytes=limit * 2**20),
        name=name,
    )(*values)
    return result if len(out) > 1 else result[0]


def pick(pieces, rows):
    width = pieces[0].shape[1]
    return in_vmem(
        functools.partial(pick_kernel, rows, CHUNKS),
        [(N * rows, width)] * CHUNKS,
        "pick",
        *pieces,
        scratch=[pltpu.VMEM((CHUNKS * N * rows, width), BF)],
        limit=16,
    )


def place(pieces, rows):
    shape = (N * rows, pieces[0].shape[1])
    return in_vmem(functools.partial(place_kernel, rows), [shape], "place", *pieces)


def silu_kernel(a_ref, b_ref, out_ref):
    for j in range(out_ref.shape[1] // 128):
        gate = pl.ds(256 * j, 128)
        up = pl.ds(256 * j + 128, 128)
        g = a_ref[:, gate].astype(F32) + b_ref[:, gate].astype(F32)
        u = a_ref[:, up].astype(F32) + b_ref[:, up].astype(F32)
        out_ref[:, pl.ds(128 * j, 128)] = (g / (1.0 + jnp.exp(-g)) * u).astype(BF)


def silu(a, b):
    return in_vmem(silu_kernel, [(a.shape[0], a.shape[1] // 2)], "silu", a, b)


def join_kernel(*refs):
    first = 0
    for ref in refs[:-1]:
        refs[-1][pl.ds(first, ref.shape[0]), :] = ref[...]
        first += ref.shape[0]


def join(*values):
    return in_vmem(join_kernel, [(sum(v.shape[0] for v in values), values[0].shape[1])], "join", *values)


def add(a, b):
    return (a.astype(F32) + b.astype(F32)).astype(BF)


def dot(a, b):
    return jnp.dot(a, b, preferred_element_type=F32).astype(BF)


def tie(*values):
    return lax.optimization_barrier(values)


def gather_tokens(t, gate_weight, up_weight):
    t1, t2, t3 = (exchange(t, z=m) for m in (1, 2, 3))
    pieces = []
    for h in join(t, t1), join(t2, t3):
        p = exchange(h, masks_x=FIRST)
        both = join(h, p)
        pieces += [h, p, exchange(both, masks_x=SECOND)]
    gate_weight, _ = tie(gate_weight, both)
    return pieces, pack(gate_weight, up_weight)


def halve(stays, got, size):
    v = add(stays, got)
    return v[:size], v[size:]


def scatter_hidden(chunks, weight, rows):
    stays, got = [None] * CHUNKS, [None] * CHUNKS

    def step(c, k, turn):
        if k == 0:
            picked = chunks[c] if turn is None else tie(chunks[c], turn)[0]
            s = dot(picked, weight)
            stays[c], sent, how = s[8 * rows :], s[: 8 * rows], dict(core=1)
        else:
            got[c], _ = tie(got[c], turn)
            if k == 4:
                stays[c] = sent = silu(stays[c], got[c])
                how = dict(zhi=1)
            else:
                size, how = [(4, dict(masks_y=FIRST)), (2, dict(masks_y=SECOND)), (1, dict(zhi=1))][k - 1]
                stays[c], sent = halve(stays[c], got[c], size * rows)
        got[c] = exchange(sent, **how)
        return sent

    turn = None
    for c, k in TURNS:
        turn = step(c, k, turn)
    return stays, got


def gather_hidden(own, other):
    halves = []
    for hidden in own, other:
        h = join(*hidden)
        h = join(h, exchange(h, masks_y=SECOND))
        halves.append(join(h, exchange(h, masks_y=FIRST)))
    return halves + [exchange(h, core=1) for h in halves]


def scatter_out(hidden, weight, rows):
    parts, stays, got = (slice(0, 512), slice(512, None)), [None, None], [None, None]
    for c, part in enumerate(parts):
        s = dot(hidden, weight[:, part])
        stays[c], turn = s[: 8 * rows], s[8 * rows :]
        got[c] = exchange(turn, masks_x=SECOND)
    for c in range(2):
        got[c], _ = tie(got[c], turn)
        stays[c], turn = halve(stays[c], got[c], 4 * rows)
        got[c] = exchange(turn, masks_x=FIRST)
    columns = []
    for c in range(2):
        if c == 1:
            got[1], z[1] = tie(got[1], z[1])
        v = add(stays[c], got[c])
        z = [v[:rows]] + [exchange(v[m * rows : (m + 1) * rows], z=m) for m in (1, 2, 3)]
        columns.append(z)
    columns = [functools.reduce(jnp.add, [p.astype(F32) for p in z]).astype(BF) for z in columns]
    return jnp.concatenate(columns, axis=1)


def shards(tokens, gate_weight, up_weight, down_weight):
    rows = tokens.shape[0]
    pieces, weight = gather_tokens(tokens, gate_weight, up_weight)
    hidden = scatter_hidden(pick(pieces, rows // CHUNKS), weight, rows // CHUNKS)
    return scatter_out(place(gather_hidden(*hidden), rows), down_weight, rows)


def solution(mesh):
    in_specs = (P("gy", "gx"), P("gx", "gy"), P("gx", "gy"), P("gy", "gx"))
    out_specs = P("gy", "gx")
    return jax.shard_map(shards, mesh=mesh, in_specs=in_specs, out_specs=out_specs, check_vma=False)
```

```python
import functools

import jax
import jax.numpy as jnp
from jax import lax
from jax.experimental import pallas as pl
from jax.experimental.pallas import tpu as pltpu
from jax.sharding import PartitionSpec as P

BF = jnp.bfloat16
F32 = jnp.float32
N = 16
CHUNKS = 3
TURNS = [(0, 0), (1, 0), (0, 1), (2, 0), (1, 1), (2, 1), (0, 2), (1, 2)]
TURNS += [(0, 3), (2, 2), (1, 3), (0, 4), (2, 3), (1, 4), (2, 4)]
FIRST = (1, 3)
SECOND = (3, 1)


def exchange(value, masks_x=(0, 0), z=0, masks_y=(0, 0), zhi=0, core=0):
    pairs = []
    for gx in range(N):
        for gy in range(N):
            other = (gx ^ (2 * masks_y[gx & 1]) ^ (8 * zhi) ^ core) * N + (gy ^ (4 * masks_x[gx & 1]) ^ z)
            pairs.append((gx * N + gy, other))
    return lax.ppermute(value, ("gx", "gy"), pairs)


def gray(v):
    return v ^ (v >> 1)


def kept(gx):
    odd = (gx & 1) == 1
    ys = [lax.select(odd, jnp.int32(gray(i)), jnp.int32(3 * gray(i) & 3)) for i in range(4)]
    return [[gx ^ (2 * y) ^ (8 * z) for z in (0, 1)] for y in ys]


def x_place(gx, block):
    return gray(lax.select((gx & 1) == 0, block >> 2, (3 * (block >> 2)) & 3))


def gathered_slot(gx, block):
    return 8 * ((block >> 1) & 1) + 2 * x_place(gx, block) + (block & 1)


def scattered_slot(gx, block):
    return 4 * x_place(gx, block) + (block & 3)


def pick_kernel(rows, n, *refs):
    pieces, outs, whole = refs[: -n - 1], refs[-n - 1 : -1], refs[-1]
    first = 0
    for piece in pieces:
        whole[pl.ds(first, piece.shape[0]), :] = piece[...]
        first += piece.shape[0]
    me = lax.axis_index("gx")
    slots = [gathered_slot(me, block) for gx in (me ^ 1, me) for blocks in kept(gx) for block in blocks]
    for chunk, out in enumerate(outs):
        for k, slot in enumerate(slots):
            source = pl.multiple_of((slot * n + chunk) * rows, 16)
            out[pl.ds(k * rows, rows), :] = whole[pl.ds(source, rows), :]


def place_kernel(rows, *refs):
    *pieces, keep_ref, send_ref, out_ref = refs
    me = lax.axis_index("gx")
    for piece, (gx, z) in zip(pieces, [(me, 0), (me, 1), (me ^ 1, 0), (me ^ 1, 1)]):
        for part, blocks in enumerate(kept(gx)):
            target = pl.multiple_of(scattered_slot(me, blocks[z]) * rows, 16)
            out_ref[pl.ds(target, rows), :] = piece[pl.ds(part * rows, rows), :]
    half = N // 2 * rows
    send_ref[...] = out_ref[half:, :]
    keep_ref[...] = out_ref[:half, :]


def pack_kernel(gate_ref, up_ref, out_ref, sems):
    copies = []
    for j in range(gate_ref.shape[1] // 128):
        for k, ref in enumerate((gate_ref, up_ref)):
            copies.append(
                pltpu.make_async_copy(
                    ref.at[:, pl.ds(128 * j, 128)], out_ref.at[:, pl.ds(256 * j + 128 * k, 128)], sems.at[2 * j + k]
                )
            )
    for copy in copies:
        copy.start()
    for copy in copies:
        copy.wait()


def pack(gate_weight, up_weight):
    width, units = gate_weight.shape
    return pl.pallas_call(
        pack_kernel,
        out_shape=jax.ShapeDtypeStruct((width, 2 * units), BF),
        in_specs=[pl.BlockSpec(memory_space=pl.ANY)] * 2,
        out_specs=pl.BlockSpec(memory_space=pltpu.VMEM),
        scratch_shapes=[pltpu.SemaphoreType.DMA((2 * units // 128,))],
        compiler_params=pltpu.CompilerParams(vmem_limit_bytes=16 * 2**20),
        cost_estimate=pl.CostEstimate(flops=0, bytes_accessed=8 * width * units, transcendentals=0),
        name="pack",
    )(gate_weight, up_weight)


def in_vmem(kernel, shapes, name, *values, scratch=(), limit=8):
    spec = pl.BlockSpec(memory_space=pltpu.VMEM)
    out = tuple(jax.ShapeDtypeStruct(shape, BF) for shape in shapes)
    result = pl.pallas_call(
        kernel,
        out_shape=out,
        in_specs=[spec] * len(values),
        out_specs=(spec,) * len(out),
        scratch_shapes=scratch,
        compiler_params=pltpu.CompilerParams(vmem_limit_bytes=limit * 2**20),
        name=name,
    )(*values)
    return result if len(out) > 1 else result[0]


def pick(pieces, rows):
    width = pieces[0].shape[1]
    return in_vmem(
        functools.partial(pick_kernel, rows, CHUNKS),
        [(N * rows, width)] * CHUNKS,
        "pick",
        *pieces,
        scratch=[pltpu.VMEM((CHUNKS * N * rows, width), BF)],
        limit=16,
    )


def place(pieces, rows):
    width = pieces[0].shape[1]
    return in_vmem(
        functools.partial(place_kernel, rows),
        [(N // 2 * rows, width)] * 2,
        "place",
        *pieces,
        scratch=[pltpu.VMEM((N * rows, width), BF)],
        limit=16,
    )


def silu_kernel(a_ref, b_ref, out_ref):
    for j in range(out_ref.shape[1] // 128):
        gate = pl.ds(256 * j, 128)
        up = pl.ds(256 * j + 128, 128)
        g = a_ref[:, gate].astype(F32) + b_ref[:, gate].astype(F32)
        u = a_ref[:, up].astype(F32) + b_ref[:, up].astype(F32)
        out_ref[:, pl.ds(128 * j, 128)] = (g / (1.0 + jnp.exp(-g)) * u).astype(BF)


def silu(a, b):
    return in_vmem(silu_kernel, [(a.shape[0], a.shape[1] // 2)], "silu", a, b)


def join_kernel(*refs):
    first = 0
    for ref in refs[:-1]:
        refs[-1][pl.ds(first, ref.shape[0]), :] = ref[...]
        first += ref.shape[0]


def join(*values):
    return in_vmem(join_kernel, [(sum(v.shape[0] for v in values), values[0].shape[1])], "join", *values)


def add(a, b):
    return (a.astype(F32) + b.astype(F32)).astype(BF)


def dot(a, b):
    return jnp.dot(a, b, preferred_element_type=F32).astype(BF)


def tie(*values):
    return lax.optimization_barrier(values)


def gather_tokens(t, gate_weight, up_weight):
    t1, t2, t3 = (exchange(t, z=m) for m in (1, 2, 3))
    pieces = []
    for h in join(t, t1), join(t2, t3):
        p = exchange(h, masks_x=FIRST)
        both = join(h, p)
        pieces += [h, p, exchange(both, masks_x=SECOND)]
    gate_weight, _ = tie(gate_weight, both)
    return pieces, pack(gate_weight, up_weight)


def halve(stays, got, size):
    v = add(stays, got)
    return v[:size], v[size:]


def scatter_hidden(chunks, weight, rows):
    stays, got = [None] * CHUNKS, [None] * CHUNKS

    def step(c, k, turn):
        if k == 0:
            picked = chunks[c] if turn is None else tie(chunks[c], turn)[0]
            s = dot(picked, weight)
            stays[c], sent, how = s[8 * rows :], s[: 8 * rows], dict(core=1)
        else:
            got[c], _ = tie(got[c], turn)
            if k == 4:
                stays[c] = sent = silu(stays[c], got[c])
                how = dict(zhi=1)
                if c == 0:
                    return sent
                if c == 1:
                    stays[0] = sent = join(stays[0], sent)
            else:
                size, how = [(4, dict(masks_y=FIRST)), (2, dict(masks_y=SECOND)), (1, dict(zhi=1))][k - 1]
                stays[c], sent = halve(stays[c], got[c], size * rows)
        got[c] = exchange(sent, **how)
        return sent

    turn = None
    for c, k in TURNS:
        turn = step(c, k, turn)
    return [stays[0], stays[2]], [got[1], got[2]]


def gather_hidden(own, other):
    halves = []
    for hidden in own, other:
        h = join(*hidden)
        h = join(h, exchange(h, masks_y=SECOND))
        halves.append(join(h, exchange(h, masks_y=FIRST)))
    return halves + [exchange(h, core=1) for h in halves]


def scatter_out(hidden, weight, rows):
    parts, stays, got = (slice(0, 512), slice(512, None)), [None, None], [None, None]
    turn = weight
    for c, part in enumerate(parts):
        first_rows, _ = tie(hidden[1], turn)
        turn = dot(first_rows, weight[:, part])
        got[c] = exchange(turn, masks_x=SECOND)
    for c, part in enumerate(parts):
        kept_rows, _ = tie(hidden[0], turn)
        (stays[c],) = tie(dot(kept_rows, weight[:, part]))
    for c in range(2):
        got[c], _ = tie(got[c], turn)
        stays[c], turn = halve(stays[c], got[c], 4 * rows)
        got[c] = exchange(turn, masks_x=FIRST)
    columns = []
    for c in range(2):
        if c == 1:
            got[1], z[1] = tie(got[1], z[1])
        v = add(stays[c], got[c])
        z = [v[:rows]] + [exchange(v[m * rows : (m + 1) * rows], z=m) for m in (1, 2, 3)]
        columns.append(z)
    columns = [functools.reduce(jnp.add, [p.astype(F32) for p in z]).astype(BF) for z in columns]
    return jnp.concatenate(columns, axis=1)


def shards(tokens, gate_weight, up_weight, down_weight):
    rows = tokens.shape[0]
    pieces, weight = gather_tokens(tokens, gate_weight, up_weight)
    hidden = scatter_hidden(pick(pieces, rows // CHUNKS), weight, rows // CHUNKS)
    return scatter_out(place(gather_hidden(*hidden), rows), down_weight, rows)


def solution(mesh):
    in_specs = (P("gy", "gx"), P("gx", "gy"), P("gx", "gy"), P("gy", "gx"))
    out_specs = P("gy", "gx")
    return jax.shard_map(shards, mesh=mesh, in_specs=in_specs, out_specs=out_specs, check_vma=False)
```

```python
import functools

import jax
import jax.numpy as jnp
from jax import lax
from jax.experimental import pallas as pl
from jax.experimental.pallas import tpu as pltpu
from jax.sharding import PartitionSpec as P

BF = jnp.bfloat16
F32 = jnp.float32
N = 16
CHUNKS = 3
TURNS = [(0, 0), (1, 0), (0, 1), (2, 0), (1, 1), (2, 1), (0, 2), (1, 2)]
TURNS += [(0, 3), (2, 2), (1, 3), (0, 4), (2, 3), (1, 4), (2, 4)]
FIRST = (1, 3)
SECOND = (3, 1)


def exchange(value, masks_x=(0, 0), z=(0, 0), masks_y=(0, 0), zhi=0, core=0):
    pairs = []
    for gx in range(N):
        for gy in range(N):
            other = (gx ^ (2 * masks_y[gx & 1]) ^ (8 * zhi) ^ core) * N + (gy ^ (4 * masks_x[gx & 1]) ^ z[gx >> 3])
            pairs.append((gx * N + gy, other))
    return lax.ppermute(value, ("gx", "gy"), pairs)


def gray(v):
    return v ^ (v >> 1)


def kept(gx):
    odd = (gx & 1) == 1
    ys = [lax.select(odd, jnp.int32(gray(i)), jnp.int32(3 * gray(i) & 3)) for i in range(4)]
    return [[gx ^ (2 * y) ^ (8 * z) for z in (0, 1)] for y in ys]


def x_place(gx, block):
    x = (block >> 1) & 3
    return gray(lax.select((gx & 1) == 0, x, (3 * x) & 3))


def gathered_slot(gx, block):
    return 8 * (block & 1) + 2 * x_place(gx, block) + (block >> 3)


def scattered_slot(gx, block):
    return 2 * x_place(gx, block) + (block & 1)


def pick_kernel(rows, n, *refs):
    pieces, outs, whole = refs[: -n - 1], refs[-n - 1 : -1], refs[-1]
    first = 0
    for piece in pieces:
        whole[pl.ds(first, piece.shape[0]), :] = piece[...]
        first += piece.shape[0]
    me = lax.axis_index("gx")
    slots = [gathered_slot(me, block) for gx in (me ^ 1, me) for blocks in kept(gx) for block in blocks]
    for chunk, out in enumerate(outs):
        for k, slot in enumerate(slots):
            source = pl.multiple_of((slot * n + chunk) * rows, 16)
            out[pl.ds(k * rows, rows), :] = whole[pl.ds(source, rows), :]


def place_kernel(rows, half, *refs):
    *pieces, keep_ref, send_ref, whole = refs
    me = lax.axis_index("gx")
    for piece, gx in zip(pieces, (me, me ^ 1)):
        for part, blocks in enumerate(kept(gx)):
            target = pl.multiple_of(scattered_slot(me, blocks[half]) * rows, 16)
            whole[pl.ds(target, rows), :] = piece[pl.ds(part * rows, rows), :]
    send_ref[...] = whole[N // 4 * rows :, :]
    keep_ref[...] = whole[: N // 4 * rows, :]


def pack_kernel(gate_ref, up_ref, out_ref, sems):
    copies = []
    for j in range(gate_ref.shape[1] // 128):
        for k, ref in enumerate((gate_ref, up_ref)):
            copies.append(
                pltpu.make_async_copy(
                    ref.at[:, pl.ds(128 * j, 128)], out_ref.at[:, pl.ds(256 * j + 128 * k, 128)], sems.at[2 * j + k]
                )
            )
    for copy in copies:
        copy.start()
    for copy in copies:
        copy.wait()


def pack(gate_weight, up_weight):
    width, units = gate_weight.shape
    return pl.pallas_call(
        pack_kernel,
        out_shape=jax.ShapeDtypeStruct((width, 2 * units), BF),
        in_specs=[pl.BlockSpec(memory_space=pl.ANY)] * 2,
        out_specs=pl.BlockSpec(memory_space=pltpu.VMEM),
        scratch_shapes=[pltpu.SemaphoreType.DMA((2 * units // 128,))],
        compiler_params=pltpu.CompilerParams(vmem_limit_bytes=16 * 2**20),
        cost_estimate=pl.CostEstimate(flops=0, bytes_accessed=8 * width * units, transcendentals=0),
        name="pack",
    )(gate_weight, up_weight)


def in_vmem(kernel, shapes, name, *values, scratch=(), limit=8):
    spec = pl.BlockSpec(memory_space=pltpu.VMEM)
    out = tuple(jax.ShapeDtypeStruct(shape, BF) for shape in shapes)
    result = pl.pallas_call(
        kernel,
        out_shape=out,
        in_specs=[spec] * len(values),
        out_specs=(spec,) * len(out),
        scratch_shapes=scratch,
        compiler_params=pltpu.CompilerParams(vmem_limit_bytes=limit * 2**20),
        name=name,
    )(*values)
    return result if len(out) > 1 else result[0]


def pick(pieces, rows):
    width = pieces[0].shape[1]
    return in_vmem(
        functools.partial(pick_kernel, rows, CHUNKS),
        [(N * rows, width)] * CHUNKS,
        "pick",
        *pieces,
        scratch=[pltpu.VMEM((CHUNKS * N * rows, width), BF)],
        limit=16,
    )


def place(pieces, rows, half):
    width = pieces[0].shape[1]
    return in_vmem(
        functools.partial(place_kernel, rows, half),
        [(N // 4 * rows, width)] * 2,
        "place",
        *pieces,
        scratch=[pltpu.VMEM((N // 2 * rows, width), BF)],
    )


def silu_kernel(a_ref, b_ref, out_ref):
    for j in range(out_ref.shape[1] // 128):
        gate = pl.ds(256 * j, 128)
        up = pl.ds(256 * j + 128, 128)
        g = a_ref[:, gate].astype(F32) + b_ref[:, gate].astype(F32)
        u = a_ref[:, up].astype(F32) + b_ref[:, up].astype(F32)
        out_ref[:, pl.ds(128 * j, 128)] = (g / (1.0 + jnp.exp(-g)) * u).astype(BF)


def silu(a, b):
    return in_vmem(silu_kernel, [(a.shape[0], a.shape[1] // 2)], "silu", a, b)


def join_kernel(*refs):
    first = 0
    for ref in refs[:-1]:
        refs[-1][pl.ds(first, ref.shape[0]), :] = ref[...]
        first += ref.shape[0]


def join(*values):
    return in_vmem(join_kernel, [(sum(v.shape[0] for v in values), values[0].shape[1])], "join", *values)


def add(a, b):
    return (a.astype(F32) + b.astype(F32)).astype(BF)


def dot(a, b):
    return jnp.dot(a, b, preferred_element_type=F32).astype(BF)


def tie(*values):
    return lax.optimization_barrier(values)


def gather_tokens(t, gate_weight, up_weight):
    t1, t2, t3 = (exchange(t, z=(m, m)) for m in (1, 2, 3))
    pieces = []
    for h in join(t, t1), join(t2, t3):
        p = exchange(h, masks_x=FIRST)
        both = join(h, p)
        pieces += [h, p, exchange(both, masks_x=SECOND)]
    gate_weight, _ = tie(gate_weight, both)
    return pieces, pack(gate_weight, up_weight)


def halve(stays, got, size):
    v = add(stays, got)
    return v[:size], v[size:]


def scatter_hidden(chunks, weight, rows):
    stays, got = [None] * CHUNKS, [None] * CHUNKS

    def step(c, k, turn):
        if k == 0:
            picked = chunks[c] if turn is None else tie(chunks[c], turn)[0]
            s = dot(picked, weight)
            stays[c], sent, how = s[8 * rows :], s[: 8 * rows], dict(core=1)
        else:
            got[c], _ = tie(got[c], turn)
            if k == 4:
                stays[c] = sent = silu(stays[c], got[c])
                how = dict(zhi=1)
                if c == 0:
                    return sent
                if c == 1:
                    stays[0] = sent = join(stays[0], sent)
            else:
                size, how = [(4, dict(masks_y=FIRST)), (2, dict(masks_y=SECOND)), (1, dict(zhi=1))][k - 1]
                stays[c], sent = halve(stays[c], got[c], size * rows)
        got[c] = exchange(sent, **how)
        return sent

    turn = None
    for c, k in TURNS:
        turn = step(c, k, turn)
    return [stays[0], stays[2]], [got[1], got[2]]


def hidden_to_output(own, other, weight, rows):
    stays = [None, None]
    hidden = [join(*own), join(*other)]
    got = [exchange(h, masks_y=SECOND) for h in hidden]
    hidden = [join(h, g) for h, g in zip(hidden, got)]
    got = tie(*[exchange(h, masks_y=FIRST) for h in hidden])
    got = list(got)
    turn = hidden[1]
    for k in range(2):
        got[k], _ = tie(got[k], turn)
        h = join(hidden[k], got[k])
        keep, send = place([h, exchange(h, core=1)], rows, k)
        turn = dot(send, weight)
        keep, _ = tie(keep, turn)
        (stays[k],) = tie(dot(keep, weight))
        got[k] = exchange(turn, masks_x=SECOND)
    for k in range(2):
        got[k], _ = tie(got[k], turn)
        stays[k], turn = halve(stays[k], got[k], 2 * rows)
        got[k] = exchange(turn, masks_x=FIRST)
    total = 0.0
    for k in range(2):
        got[k], _ = tie(got[k], turn)
        v = turn = add(stays[k], got[k])
        first, second = ((0, 1), (2, 3)) if k == 0 else ((1, 0), (3, 2))
        total += exchange(v[rows:], z=second).astype(F32) + exchange(v[:rows], z=first).astype(F32)
    return total.astype(BF)


def shards(tokens, gate_weight, up_weight, down_weight):
    rows = tokens.shape[0]
    pieces, weight = gather_tokens(tokens, gate_weight, up_weight)
    own, other = scatter_hidden(pick(pieces, rows // CHUNKS), weight, rows // CHUNKS)
    return hidden_to_output(own, other, down_weight, rows)


def solution(mesh):
    in_specs = (P("gy", "gx"), P("gx", "gy"), P("gx", "gy"), P("gy", "gx"))
    out_specs = P("gy", "gx")
    return jax.shard_map(shards, mesh=mesh, in_specs=in_specs, out_specs=out_specs, check_vma=False)
```

```python
import functools

import jax
import jax.numpy as jnp
from jax import lax
from jax.experimental import pallas as pl
from jax.experimental.pallas import tpu as pltpu
from jax.sharding import PartitionSpec as P

BF = jnp.bfloat16
F32 = jnp.float32
N = 16
CHUNKS = 3
TURNS = [(0, 0), (1, 0), (0, 1), (2, 0), (1, 1), (2, 1), (0, 2), (1, 2)]
TURNS += [(0, 3), (2, 2), (1, 3), (0, 4), (2, 3), (1, 4), (2, 4)]
FIRST = (1, 3)
SECOND = (3, 1)


def exchange(value, masks_x=(0, 0), z=(0, 0), masks_y=(0, 0), zhi=0, core=0):
    pairs = []
    for gx in range(N):
        for gy in range(N):
            other = (gx ^ (2 * masks_y[gx & 1]) ^ (8 * zhi) ^ core) * N + (gy ^ (4 * masks_x[gx & 1]) ^ z[gx >> 3])
            pairs.append((gx * N + gy, other))
    return lax.ppermute(value, ("gx", "gy"), pairs)


def gray(v):
    return v ^ (v >> 1)


def kept(gx):
    odd = (gx & 1) == 1
    ys = [lax.select(odd, jnp.int32(gray(i)), jnp.int32(3 * gray(i) & 3)) for i in range(4)]
    return [[gx ^ (2 * y) ^ (8 * z) for z in (0, 1)] for y in ys]


def x_place(gx, block):
    x = (block >> 1) & 3
    return gray(lax.select((gx & 1) == 0, x, (3 * x) & 3))


def gathered_slot(gx, block):
    return 8 * (block & 1) + 2 * x_place(gx, block) + (block >> 3)


def scattered_slot(gx, block):
    return 2 * x_place(gx, block) + (block & 1)


def pick_kernel(rows, n, *refs):
    pieces, outs, whole = refs[: -n - 1], refs[-n - 1 : -1], refs[-1]
    first = 0
    for piece in pieces:
        whole[pl.ds(first, piece.shape[0]), :] = piece[...]
        first += piece.shape[0]
    me = lax.axis_index("gx")
    slots = [gathered_slot(me, block) for gx in (me ^ 1, me) for blocks in kept(gx) for block in blocks]
    for chunk, out in enumerate(outs):
        for k, slot in enumerate(slots):
            source = pl.multiple_of((slot * n + chunk) * rows, 16)
            out[pl.ds(k * rows, rows), :] = whole[pl.ds(source, rows), :]


def place_kernel(rows, half, *refs):
    *pieces, keep_ref, send_ref, whole = refs
    me = lax.axis_index("gx")
    for piece, gx in zip(pieces, (me, me ^ 1)):
        for part, blocks in enumerate(kept(gx)):
            target = pl.multiple_of(scattered_slot(me, blocks[half]) * rows, 16)
            whole[pl.ds(target, rows), :] = piece[pl.ds(part * rows, rows), :]
    send_ref[...] = whole[N // 4 * rows :, :]
    keep_ref[...] = whole[: N // 4 * rows, :]


def pack_kernel(gate_ref, up_ref, out_ref, sems):
    copies = []
    for j in range(gate_ref.shape[1] // 128):
        for k, ref in enumerate((gate_ref, up_ref)):
            copies.append(
                pltpu.make_async_copy(
                    ref.at[:, pl.ds(128 * j, 128)], out_ref.at[:, pl.ds(256 * j + 128 * k, 128)], sems.at[2 * j + k]
                )
            )
    for copy in copies:
        copy.start()
    for copy in copies:
        copy.wait()


def pack(gate_weight, up_weight):
    width, units = gate_weight.shape
    return pl.pallas_call(
        pack_kernel,
        out_shape=jax.ShapeDtypeStruct((width, 2 * units), BF),
        in_specs=[pl.BlockSpec(memory_space=pl.ANY)] * 2,
        out_specs=pl.BlockSpec(memory_space=pltpu.VMEM),
        scratch_shapes=[pltpu.SemaphoreType.DMA((2 * units // 128,))],
        compiler_params=pltpu.CompilerParams(vmem_limit_bytes=16 * 2**20),
        cost_estimate=pl.CostEstimate(flops=0, bytes_accessed=8 * width * units, transcendentals=0),
        name="pack",
    )(gate_weight, up_weight)


def in_vmem(kernel, shapes, name, *values, scratch=(), limit=8):
    spec = pl.BlockSpec(memory_space=pltpu.VMEM)
    out = tuple(jax.ShapeDtypeStruct(shape, BF) for shape in shapes)
    result = pl.pallas_call(
        kernel,
        out_shape=out,
        in_specs=[spec] * len(values),
        out_specs=(spec,) * len(out),
        scratch_shapes=scratch,
        compiler_params=pltpu.CompilerParams(vmem_limit_bytes=limit * 2**20),
        name=name,
    )(*values)
    return result if len(out) > 1 else result[0]


def pick(pieces, rows):
    width = pieces[0].shape[1]
    return in_vmem(
        functools.partial(pick_kernel, rows, CHUNKS),
        [(N * rows, width)] * CHUNKS,
        "pick",
        *pieces,
        scratch=[pltpu.VMEM((CHUNKS * N * rows, width), BF)],
        limit=16,
    )


def place(pieces, rows, half):
    width = pieces[0].shape[1]
    return in_vmem(
        functools.partial(place_kernel, rows, half),
        [(N // 4 * rows, width)] * 2,
        "place",
        *pieces,
        scratch=[pltpu.VMEM((N // 2 * rows, width), BF)],
    )


def silu_kernel(a_ref, b_ref, out_ref):
    for j in range(out_ref.shape[1] // 128):
        gate = pl.ds(256 * j, 128)
        up = pl.ds(256 * j + 128, 128)
        g = a_ref[:, gate].astype(F32) + b_ref[:, gate].astype(F32)
        u = a_ref[:, up].astype(F32) + b_ref[:, up].astype(F32)
        out_ref[:, pl.ds(128 * j, 128)] = (g / (1.0 + jnp.exp(-g)) * u).astype(BF)


def silu(a, b):
    return in_vmem(silu_kernel, [(a.shape[0], a.shape[1] // 2)], "silu", a, b)


def join_kernel(*refs):
    first = 0
    for ref in refs[:-1]:
        refs[-1][pl.ds(first, ref.shape[0]), :] = ref[...]
        first += ref.shape[0]


def join(*values):
    return in_vmem(join_kernel, [(sum(v.shape[0] for v in values), values[0].shape[1])], "join", *values)


def add(a, b):
    return (a.astype(F32) + b.astype(F32)).astype(BF)


def dot(a, b):
    return jnp.dot(a, b, preferred_element_type=F32).astype(BF)


def tie(*values):
    return lax.optimization_barrier(values)


def gather_tokens(t, gate_weight, up_weight):
    t1, t2, t3 = (exchange(t, z=(m, m)) for m in (1, 2, 3))
    pieces = []
    for h in join(t, t1), join(t2, t3):
        p = exchange(h, masks_x=FIRST)
        both = join(h, p)
        pieces += [h, p, exchange(both, masks_x=SECOND)]
    gate_weight, _ = tie(gate_weight, both)
    return pieces, pack(gate_weight, up_weight)


def halve(stays, got, size):
    v = add(stays, got)
    return v[:size], v[size:]


def scatter_hidden(chunks, weight, rows):
    stays, got = [None] * CHUNKS, [None] * CHUNKS

    def step(c, k, turn):
        if k == 0:
            picked = chunks[c] if turn is None else tie(chunks[c], turn)[0]
            s = dot(picked, weight)
            stays[c], sent, how = s[8 * rows :], s[: 8 * rows], dict(core=1)
        else:
            got[c], _ = tie(got[c], turn)
            if k == 4:
                stays[c] = sent = silu(stays[c], got[c])
                how = dict(zhi=1)
                if c == 0:
                    return sent
                if c == 1:
                    stays[0] = sent = join(stays[0], sent)
            else:
                size, how = [(4, dict(masks_y=FIRST)), (2, dict(masks_y=SECOND)), (1, dict(zhi=1))][k - 1]
                stays[c], sent = halve(stays[c], got[c], size * rows)
        got[c] = exchange(sent, **how)
        return sent

    turn = None
    for c, k in TURNS:
        turn = step(c, k, turn)
    return [stays[0], stays[2]], [got[1], got[2]]


def hidden_to_output(own, other, weight, rows):
    stays = [None, None]
    hidden = [join(*own), join(*other)]
    got = [exchange(h, masks_y=SECOND) for h in hidden]
    hidden = [join(h, g) for h, g in zip(hidden, got)]
    got = [exchange(h, masks_y=FIRST) for h in hidden]
    hidden = [join(h, g) for h, g in zip(hidden, got)]
    got = list(tie(*[exchange(h, core=1) for h in hidden]))
    for k in range(2):
        if k == 1:
            got[1], _ = tie(got[1], turn)
        keep, send = place([hidden[k], got[k]], rows, k)
        turn = dot(send, weight)
        keep, _ = tie(keep, turn)
        (stays[k],) = tie(dot(keep, weight))
        got[k] = exchange(turn, masks_x=SECOND)
    for k in range(2):
        got[k], _ = tie(got[k], turn)
        if k == 1:
            got[1], got[0] = tie(got[1], got[0])
        stays[k], turn = halve(stays[k], got[k], 2 * rows)
        got[k] = exchange(turn, masks_x=FIRST)
    total = 0.0
    for k in range(2):
        got[k], _ = tie(got[k], turn)
        v = turn = add(stays[k], got[k])
        first, second = ((0, 1), (2, 3)) if k == 0 else ((1, 0), (3, 2))
        total += exchange(v[rows:], z=second).astype(F32) + exchange(v[:rows], z=first).astype(F32)
    return total.astype(BF)


def shards(tokens, gate_weight, up_weight, down_weight):
    rows = tokens.shape[0]
    pieces, weight = gather_tokens(tokens, gate_weight, up_weight)
    own, other = scatter_hidden(pick(pieces, rows // CHUNKS), weight, rows // CHUNKS)
    return hidden_to_output(own, other, down_weight, rows)


def solution(mesh):
    in_specs = (P("gy", "gx"), P("gx", "gy"), P("gx", "gy"), P("gy", "gx"))
    out_specs = P("gy", "gx")
    return jax.shard_map(shards, mesh=mesh, in_specs=in_specs, out_specs=out_specs, check_vma=False)
```

```python
import functools

import jax
import jax.numpy as jnp
from jax import lax
from jax.experimental import pallas as pl
from jax.experimental.pallas import tpu as pltpu
from jax.sharding import PartitionSpec as P

BF = jnp.bfloat16
F32 = jnp.float32
N = 16
CHUNKS = 3
TURNS = [(0, 0), (1, 0), (0, 1), (2, 0), (1, 1), (2, 1), (0, 2), (1, 2)]
TURNS += [(0, 3), (2, 2), (1, 3), (0, 4), (2, 3), (1, 4), (2, 4)]
FIRST = (1, 3)
SECOND = (3, 1)


def exchange(value, masks_x=(0, 0), z=0, masks_y=(0, 0), zhi=0, core=0):
    pairs = []
    for gx in range(N):
        for gy in range(N):
            other = (gx ^ (2 * masks_y[gx & 1]) ^ (8 * zhi) ^ core) * N + (gy ^ (4 * masks_x[gx & 1]) ^ z)
            pairs.append((gx * N + gy, other))
    return lax.ppermute(value, ("gx", "gy"), pairs)


def gray(v):
    return v ^ (v >> 1)


def kept(gx):
    odd = (gx & 1) == 1
    ys = [lax.select(odd, jnp.int32(gray(i)), jnp.int32(3 * gray(i) & 3)) for i in range(4)]
    return [[gx ^ (2 * y) ^ (8 * z) for z in (0, 1)] for y in ys]


def x_place(gx, block):
    return gray(lax.select((gx & 1) == 0, block >> 2, (3 * (block >> 2)) & 3))


def gathered_slot(gx, block):
    return 8 * ((block >> 1) & 1) + 2 * x_place(gx, block) + (block & 1)


def scattered_slot(gx, block):
    return 4 * x_place(gx, block) + (block & 3)


def pick_kernel(rows, n, *refs):
    pieces, outs, whole = refs[: -n - 1], refs[-n - 1 : -1], refs[-1]
    first = 0
    for piece in pieces:
        whole[pl.ds(first, piece.shape[0]), :] = piece[...]
        first += piece.shape[0]
    me = lax.axis_index("gx")
    slots = [gathered_slot(me, block) for gx in (me ^ 1, me) for blocks in kept(gx) for block in blocks]
    for chunk, out in enumerate(outs):
        for k, slot in enumerate(slots):
            source = pl.multiple_of((slot * n + chunk) * rows, 16)
            out[pl.ds(k * rows, rows), :] = whole[pl.ds(source, rows), :]


def place_kernel(rows, *refs):
    *pieces, keep_ref, send_ref, out_ref = refs
    me = lax.axis_index("gx")
    for piece, (gx, z) in zip(pieces, [(me, 0), (me, 1), (me ^ 1, 0), (me ^ 1, 1)]):
        for part, blocks in enumerate(kept(gx)):
            target = pl.multiple_of(scattered_slot(me, blocks[z]) * rows, 16)
            out_ref[pl.ds(target, rows), :] = piece[pl.ds(part * rows, rows), :]
    half = N // 2 * rows
    send_ref[...] = out_ref[half:, :]
    keep_ref[...] = out_ref[:half, :]


def pack_kernel(gate_ref, up_ref, out_ref, sems):
    copies = []
    for j in range(gate_ref.shape[1] // 128):
        for k, ref in enumerate((gate_ref, up_ref)):
            copies.append(
                pltpu.make_async_copy(
                    ref.at[:, pl.ds(128 * j, 128)], out_ref.at[:, pl.ds(256 * j + 128 * k, 128)], sems.at[2 * j + k]
                )
            )
    for copy in copies:
        copy.start()
    for copy in copies:
        copy.wait()


def pack(gate_weight, up_weight):
    width, units = gate_weight.shape
    return pl.pallas_call(
        pack_kernel,
        out_shape=jax.ShapeDtypeStruct((width, 2 * units), BF),
        in_specs=[pl.BlockSpec(memory_space=pl.ANY)] * 2,
        out_specs=pl.BlockSpec(memory_space=pltpu.VMEM),
        scratch_shapes=[pltpu.SemaphoreType.DMA((2 * units // 128,))],
        compiler_params=pltpu.CompilerParams(vmem_limit_bytes=16 * 2**20),
        cost_estimate=pl.CostEstimate(flops=0, bytes_accessed=8 * width * units, transcendentals=0),
        name="pack",
    )(gate_weight, up_weight)


def in_vmem(kernel, shapes, name, *values, scratch=(), limit=8):
    spec = pl.BlockSpec(memory_space=pltpu.VMEM)
    out = tuple(jax.ShapeDtypeStruct(shape, BF) for shape in shapes)
    result = pl.pallas_call(
        kernel,
        out_shape=out,
        in_specs=[spec] * len(values),
        out_specs=(spec,) * len(out),
        scratch_shapes=scratch,
        compiler_params=pltpu.CompilerParams(vmem_limit_bytes=limit * 2**20),
        name=name,
    )(*values)
    return result if len(out) > 1 else result[0]


def pick(pieces, rows):
    width = pieces[0].shape[1]
    return in_vmem(
        functools.partial(pick_kernel, rows, CHUNKS),
        [(N * rows, width)] * CHUNKS,
        "pick",
        *pieces,
        scratch=[pltpu.VMEM((CHUNKS * N * rows, width), BF)],
        limit=16,
    )


def place(pieces, rows):
    width = pieces[0].shape[1]
    return in_vmem(
        functools.partial(place_kernel, rows),
        [(N // 2 * rows, width)] * 2,
        "place",
        *pieces,
        scratch=[pltpu.VMEM((N * rows, width), BF)],
        limit=16,
    )


def silu_kernel(a_ref, b_ref, out_ref):
    for j in range(out_ref.shape[1] // 128):
        gate = pl.ds(256 * j, 128)
        up = pl.ds(256 * j + 128, 128)
        g = a_ref[:, gate].astype(F32) + b_ref[:, gate].astype(F32)
        u = a_ref[:, up].astype(F32) + b_ref[:, up].astype(F32)
        out_ref[:, pl.ds(128 * j, 128)] = (g / (1.0 + jnp.exp(-g)) * u).astype(BF)


def silu(a, b):
    return in_vmem(silu_kernel, [(a.shape[0], a.shape[1] // 2)], "silu", a, b)


def join_kernel(*refs):
    first = 0
    for ref in refs[:-1]:
        refs[-1][pl.ds(first, ref.shape[0]), :] = ref[...]
        first += ref.shape[0]


def join(*values):
    return in_vmem(join_kernel, [(sum(v.shape[0] for v in values), values[0].shape[1])], "join", *values)


def add(a, b):
    return (a.astype(F32) + b.astype(F32)).astype(BF)


def dot(a, b):
    return jnp.dot(a, b, preferred_element_type=F32).astype(BF)


def tie(*values):
    return lax.optimization_barrier(values)


def gather_tokens(t, gate_weight, up_weight):
    t1, t2, t3 = (exchange(t, z=m) for m in (1, 2, 3))
    pieces = []
    for h in join(t, t1), join(t2, t3):
        p = exchange(h, masks_x=FIRST)
        both = join(h, p)
        pieces += [h, p, exchange(both, masks_x=SECOND)]
    gate_weight, _ = tie(gate_weight, both)
    return pieces, pack(gate_weight, up_weight)


def halve(stays, got, size):
    v = add(stays, got)
    return v[:size], v[size:]


def scatter_hidden(chunks, weight, rows):
    stays, got = [None] * CHUNKS, [None] * CHUNKS

    def step(c, k, turn):
        if k == 0:
            picked = chunks[c] if turn is None else tie(chunks[c], turn)[0]
            s = dot(picked, weight)
            stays[c], sent, how = s[8 * rows :], s[: 8 * rows], dict(core=1)
        else:
            got[c], _ = tie(got[c], turn)
            if k == 4:
                stays[c] = sent = silu(stays[c], got[c])
                how = dict(zhi=1)
                if c == 0:
                    return sent
                if c == 1:
                    stays[0] = sent = join(stays[0], sent)
            else:
                size, how = [(4, dict(masks_y=FIRST)), (2, dict(masks_y=SECOND)), (1, dict(zhi=1))][k - 1]
                stays[c], sent = halve(stays[c], got[c], size * rows)
        got[c] = exchange(sent, **how)
        return sent

    turn = None
    for c, k in TURNS:
        turn = step(c, k, turn)
    return [stays[0], stays[2]], [got[1], got[2]]


def gather_hidden(own, other):
    halves = []
    for hidden in own, other:
        h = join(*hidden)
        h = join(h, exchange(h, masks_y=SECOND))
        halves.append(join(h, exchange(h, masks_y=FIRST)))
    return halves + [exchange(h, core=1) for h in halves]


def scatter_out(hidden, weight, rows):
    parts, stays, got = (slice(0, 640), slice(640, None)), [None, None], [None, None]
    turn = weight
    for c, part in enumerate(parts):
        first_rows, _ = tie(hidden[1], turn)
        turn = dot(first_rows, weight[:, part])
        got[c] = exchange(turn, masks_x=SECOND)
    for c, part in enumerate(parts):
        kept_rows, _ = tie(hidden[0], turn)
        (stays[c],) = tie(dot(kept_rows, weight[:, part]))
    for c in range(2):
        got[c], _ = tie(got[c], turn)
        stays[c], turn = halve(stays[c], got[c], 4 * rows)
        got[c] = exchange(turn, masks_x=FIRST)
    columns = []
    for c in range(2):
        if c == 1:
            got[1], z[1] = tie(got[1], z[1])
        v = add(stays[c], got[c])
        z = [v[:rows]] + [exchange(v[m * rows : (m + 1) * rows], z=m) for m in (1, 2, 3)]
        columns.append(z)
    columns = [functools.reduce(jnp.add, [p.astype(F32) for p in z]).astype(BF) for z in columns]
    return jnp.concatenate(columns, axis=1)


def shards(tokens, gate_weight, up_weight, down_weight):
    rows = tokens.shape[0]
    pieces, weight = gather_tokens(tokens, gate_weight, up_weight)
    hidden = scatter_hidden(pick(pieces, rows // CHUNKS), weight, rows // CHUNKS)
    return scatter_out(place(gather_hidden(*hidden), rows), down_weight, rows)


def solution(mesh):
    in_specs = (P("gy", "gx"), P("gx", "gy"), P("gx", "gy"), P("gy", "gx"))
    out_specs = P("gy", "gx")
    return jax.shard_map(shards, mesh=mesh, in_specs=in_specs, out_specs=out_specs, check_vma=False)
```
